256 devices in a mesh: island: 16 (over y_hi, x, core), fsdp: 16 (over z, y_lo).
Axes of the slice: x: 4, y: 4 (y_hi: 2, y_lo: 2; y = y_hi * 2 + y_lo), z: 8, core: 2. Of those that a mesh axis runs over, the one named last changes fastest.
Arguments:
- context: bfloat16 [65536, 2048], P(('island', 'fsdp')), may hold values from -24 to 24
- cotangent: bfloat16 [65536, 2048], P(('island', 'fsdp')), may hold values from -6 to 6
- norm_gain: float32 [2048], replicated, may hold values from 0.1 to 1.9
- out_weight: bfloat16 [16, 2048, 2048], P('island', 'fsdp'), may hold values from -4 to 4
- moment_one: float32 [16, 2048, 2048], P('island', 'fsdp'), may hold values from -3 to 3
- moment_two: float32 [16, 2048, 2048], P('island', 'fsdp'), may hold values from 0.05 to 2
- local_frags: bfloat16 [16, 2, 2048, 2048], P('island', None, 'fsdp'), may hold values from -5 to 5
- anchors: bfloat16 [2, 2048, 2048], P(None, 'fsdp'), may hold values from -5 to 5
- outer_moment: float32 [2, 2048, 2048], P(None, 'fsdp'), may hold values from -3 to 3
- outer_step: int32 [1], replicated, may hold values from 0 to 999
Outputs:
- context_grad: bfloat16 [65536, 2048], P(('island', 'fsdp'))
- weight_new: bfloat16 [16, 2048, 2048], P('island', 'fsdp')
- moment_one_new: float32 [16, 2048, 2048], P('island', 'fsdp')
- moment_two_new: float32 [16, 2048, 2048], P('island', 'fsdp')
- anchor_new: bfloat16 [2048, 2048], P('fsdp')
- outer_moment_new: float32 [2048, 2048], P('fsdp')
The draws below stay inside these ranges and needn't reach their ends.
All inputs are finite; a program needn't handle non-finite values.
Results may differ from the reference program's by a relative error of at most 0.017.
Values may be sent and summed in bfloat16 or wider, within the bound.
A program may use at most 128 MiB of HBM per device.

```python
import math
import jax
import jax.numpy as jnp
from jax import lax

D = 2048
NFRAG = 2
K = 2048
TOK_ISL = 4096
TOKENS = 65536
N_ISLAND = 16


def raised(array, own_key, source, target, blocks, factor):
    def block_of(axis_at):
        return (jnp.arange(array.shape[axis_at]) // (array.shape[axis_at] // blocks)).reshape((-1,) + (1,) * (array.ndim - 1 - axis_at))

    first = jax.random.permutation(own_key, blocks)[block_of(target)]
    far = (block_of(target) + blocks // 2) % blocks
    return jnp.where((block_of(source) == first) | (block_of(source) == far), factor * array, array)


def block_scale(stream_key, extent, split, least, top_value):
    factor_of, own = 1.0, jax.random.fold_in(stream_key, 6)
    for axis_at, parts in split:
        draws = jnp.exp(jax.random.uniform(jax.random.fold_in(own, axis_at), (parts,), jnp.float32, least / len(split), top_value / len(split)))
        factor_of = factor_of * jnp.repeat(draws, extent[axis_at] // parts).reshape([-1 if axis == axis_at else 1 for axis in range(len(extent))])
    return factor_of


def scatter_about(own_key, shape, spread, bound, split=(), dtype=jnp.bfloat16):
    drawn = jax.random.normal(own_key, shape, jnp.float32) * spread
    if len(split) > 0:
        drawn = block_scale(own_key, shape, split, -0.22, 0.18) * drawn
    return jnp.clip(drawn, min=-bound, max=bound).astype(dtype)


def gaussian_with(key, shape, deviation, reach, pieces, heavy, kind=jnp.bfloat16):
    result = deviation * jax.random.normal(key, shape, jnp.float32)
    if pieces:
        result = result * block_scale(key, shape, pieces, -0.22, 0.18)
    return jnp.clip(raised(result, jax.random.fold_in(key, 3), *heavy), -reach, reach).astype(kind)


def setup_inputs(seed: int = 0) -> dict:
    keys = jax.random.split(jax.random.key(seed), 11)
    return {
        "context": gaussian_with(keys[0], (TOKENS, K), 1.0, 24.0, ((0, 256),), (0, 1, 256, 6.0)),
        "cotangent": scatter_about(keys[1], (TOKENS, D), 1.0, 6.0, ((0, 256),)),
        "norm_gain": jnp.clip(1.0 + 0.18 * jax.random.normal(keys[2], (D,), jnp.float32), 0.1, 1.9),
        "out_weight": scatter_about(keys[3], (N_ISLAND, K, D), 1.0, 4.0, ((0, 16), (1, 16))),
        "moment_one": scatter_about(keys[4], (N_ISLAND, K, D), 0.5, 3.0, ((0, 16), (1, 16)), jnp.float32),
        "moment_two": jnp.clip(jnp.exp(math.log(2.0) - 3.6888794 * jax.random.uniform(keys[5], (N_ISLAND, K, D), jnp.float32) ** block_scale(keys[5], (N_ISLAND, K, D), ((0, 16), (1, 16)), -0.2, 0.2)), 0.05, 2.0),
        "local_frags": scatter_about(keys[6], (N_ISLAND, NFRAG, K, D), 1.0, 5.0, ((0, 16), (2, 16))),
        "anchors": scatter_about(keys[7], (NFRAG, K, D), 1.0, 5.0, ((1, 16),)),
        "outer_moment": scatter_about(keys[8], (NFRAG, K, D), 0.5, 3.0, ((1, 16),), jnp.float32),
        "outer_step": jax.random.randint(keys[9], (1,), 0, 1000).astype(jnp.int32),
    }


beta_one = 0.9
beta_two = 0.95
inner_rate = 0.01
decay_rate = 0.1
adam_eps = 1e-08
outer_mu = 0.9
rate_base = 0.35

def island_step(context_i, cot_i, norm_gain, weight_i, first_i, second_i):
    projected = jnp.dot(context_i, weight_i, preferred_element_type=jnp.float32)
    inv_rms = lax.rsqrt(lax.optimization_barrier(jnp.mean(projected * projected, axis=-1, keepdims=True)) + 1e-06)
    scaled_cot = cot_i.astype(jnp.float32) * norm_gain
    inner = lax.optimization_barrier(jnp.mean(scaled_cot * projected, axis=-1, keepdims=True))
    proj_grad = (inv_rms * (scaled_cot - projected * inv_rms * inv_rms * inner)).astype(jnp.bfloat16)
    ctx_grad = jnp.dot(proj_grad, weight_i.T, preferred_element_type=jnp.float32).astype(jnp.bfloat16)
    weight_grad = jnp.dot(context_i.T, proj_grad, preferred_element_type=jnp.float32)
    first_new = beta_one * first_i + (1.0 - beta_one) * weight_grad
    second_new = beta_two * second_i + (1.0 - beta_two) * weight_grad * weight_grad
    weight_f = weight_i.astype(jnp.float32)
    update = first_new / (jnp.sqrt(second_new) + adam_eps) + decay_rate * weight_f
    new_weight = (weight_f - inner_rate * update).astype(jnp.bfloat16)
    return (ctx_grad, new_weight, first_new, second_new)

def reference(context, cotangent, norm_gain, out_weight, moment_one, moment_two, local_frags, anchors, outer_moment, outer_step):
    ctx_all = context.reshape(N_ISLAND, TOK_ISL, K)
    cot_all = cotangent.reshape(N_ISLAND, TOK_ISL, D)

    def one_island(items):
        return island_step(items[0], items[1], norm_gain, items[2], items[3], items[4])
    ctx_grad, new_weight, first_new, second_new = lax.map(one_island, (ctx_all, cot_all, out_weight, moment_one, moment_two))
    due_index = (outer_step[0] % NFRAG).astype(jnp.int32)
    step_rate = rate_base + rate_base * jnp.minimum(outer_step[0], 1000).astype(jnp.float32) / 1000.0
    local_due = lax.dynamic_index_in_dim(local_frags, due_index, 1, keepdims=False).astype(jnp.float32)
    anchor_due = lax.dynamic_index_in_dim(anchors, due_index, 0, keepdims=False).astype(jnp.float32)
    moment_due = lax.dynamic_index_in_dim(outer_moment, due_index, 0, keepdims=False)
    pseudo = anchor_due - lax.optimization_barrier(jnp.sum(local_due, axis=0)) / N_ISLAND
    moment_new = outer_mu * moment_due + pseudo
    anchor_new = (anchor_due - step_rate * (pseudo + outer_mu * moment_new)).astype(jnp.bfloat16)
    return (ctx_grad.reshape(TOKENS, K), new_weight, first_new, second_new, anchor_new, moment_new)
```

```python
import functools

import jax
import jax.numpy as jnp
from jax import lax
from jax.experimental import pallas as pl
from jax.experimental.pallas import tpu as pltpu
from jax.sharding import PartitionSpec as P

NFRAG = 2

beta_one = 0.9
beta_two = 0.95
inner_rate = 0.01
decay_rate = 0.1
adam_eps = 1e-08
outer_mu = 0.9
rate_base = 0.35

NZ = 8
TOK = 256
PAIR = 512
D = 2048
HALF = 1024
ROWS = 128
CHUNK = 256
UNIT = 64

F32 = jnp.float32
BF16 = jnp.bfloat16
MESH = pl.DeviceIdType.MESH


def aligned(value, size):
    return pl.multiple_of(value * size, size)


def kernel(
    ctx_hbm,
    cot_hbm,
    gain_ref,
    w_hbm,
    frag_hbm,
    step_ref,
    cg_hbm,
    grad_hbm,
    drift_hbm,
    wbuf,
    ctx,
    cot,
    proj,
    pg,
    ctxt,
    stat_own,
    stat_send,
    stat_recv,
    far,
    parts,
    half_send,
    half_recv,
    full_send,
    full_recv,
    y_send,
    y_recv,
    grad_out,
    cg_own,
    cg_send,
    cg_recv,
    cg_out,
    frag,
    sel,
    sum_a,
    sum_b,
    sum_c,
    pass_a,
    pass_b,
    pass_c,
    got_a,
    got_b,
    got_c,
    got_d,
    drift,
    loc_sem,
    out_sem,
    zs_sem,
    zr_sem,
    ys_sem,
    yr_sem,
    hs_sem,
    hr_sem,
    fs_sem,
    fr_sem,
    as_sem,
    ar_sem,
):
    isl = lax.axis_index("island")
    fsd = lax.axis_index("fsdp")
    y = lax.rem(fsd, 2)
    z = lax.div(fsd, 2)
    core = lax.rem(isl, 2)
    x = lax.rem(lax.div(isl, 2), 4)
    yh = lax.div(isl, 8)
    xa = lax.rem(x, 2)
    xb = lax.div(x, 2)
    other = 1 - y
    up = (isl, lax.rem(z + 1, NZ) * 2 + y)
    down = (isl, lax.rem(z + NZ - 1, NZ) * 2 + y)
    ring = (up, down)
    pair = (isl, z * 2 + other)
    sib = (isl + 1 - 2 * core, fsd)
    near_x = (isl + 2 - 4 * xa, fsd)
    far_x = (isl + 4 - 8 * xb, fsd)
    far_y = (isl + 8 - 16 * yh, fsd)
    mine = aligned(y, HALF)
    theirs = aligned(other, HALF)

    sends = []

    def send(src, dst, ss, rs, dev):
        copy = pltpu.make_async_remote_copy(
            src_ref=src, dst_ref=dst, send_sem=ss, recv_sem=rs, device_id=dev, device_id_type=MESH
        )
        copy.start()
        sends.append(copy)

    def arrive(dst, ss, rs):
        pltpu.make_async_remote_copy(
            src_ref=dst, dst_ref=dst, send_sem=ss, recv_sem=rs, device_id=pair, device_id_type=MESH
        ).wait_recv()

    loc_w = pltpu.make_async_copy(
        w_hbm.at[0, :, pl.ds(mine, HALF)], wbuf.at[pl.ds(aligned(fsd, ROWS), ROWS), :], loc_sem.at[0]
    )
    loc_ctx = pltpu.make_async_copy(ctx_hbm, ctx.at[pl.ds(0, TOK), :], loc_sem.at[1])
    loc_cot = pltpu.make_async_copy(
        cot_hbm.at[:, pl.ds(mine, HALF)], cot.at[pl.ds(0, TOK), :], loc_sem.at[2]
    )
    loc_frag = pltpu.make_async_copy(frag_hbm.at[0], frag, loc_sem.at[3])
    for copy in (loc_w, loc_frag, loc_ctx, loc_cot):
        copy.start()

    barrier = pltpu.get_barrier_semaphore()
    for dev in (up, down, pair, sib, near_x, far_x, far_y):
        pl.semaphore_signal(barrier, inc=1, device_id=dev, device_id_type=MESH)
    pl.semaphore_wait(barrier, 7)

    def unit_rows(z_from, u):
        owner = y if u < 2 else other
        return pl.ds(pl.multiple_of(z_from * CHUNK + owner * ROWS + (u % 2) * UNIT, UNIT), UNIT)

    for t in range(2):
        rows = pl.ds(t * UNIT, UNIT)
        send(
            w_hbm.at[0, rows, pl.ds(theirs, HALF)],
            wbuf.at[unit_rows(z, t), :],
            ys_sem.at[t],
            yr_sem.at[t],
            pair,
        )
        for way in range(2):
            send(
                w_hbm.at[0, rows, pl.ds(mine, HALF)],
                wbuf.at[unit_rows(z, t), :],
                zs_sem.at[way, 0, t],
                zr_sem.at[way, 0, t],
                ring[way],
            )

    def pass_on(hop, u, way, z_from):
        if hop < 3 or (u % 2) == way:
            ref = wbuf.at[unit_rows(z_from, u), :]
            send(ref, ref, zs_sem.at[way, hop, u], zr_sem.at[way, hop, u], ring[way])

    for t in range(2):
        arrive(wbuf.at[unit_rows(z, 2 + t), :], ys_sem.at[t], yr_sem.at[t])
        for way in range(2):
            pass_on(0, 2 + t, way, z)

    send(ctx_hbm, ctx.at[pl.ds(TOK, TOK), :], ys_sem.at[2], yr_sem.at[2], pair)
    send(
        cot_hbm.at[:, pl.ds(theirs, HALF)],
        cot.at[pl.ds(TOK, TOK), :],
        ys_sem.at[3],
        yr_sem.at[3],
        pair,
    )

    row_a = core * 64
    row_b = row_a + xa * 32
    row_c = row_b + xb * 16

    def rows_of(start, size):
        return pl.ds(pl.multiple_of(start, size), size)

    def outer_0():
        loc_frag.wait()
        due = jnp.full((16, D), jnp.bitwise_and(step_ref[0], 1), jnp.int32)

        @pl.loop(0, 8)
        def _(r):
            rows = rows_of(r * 16, 16)
            sel[rows, :] = jnp.where(
                due == 0, frag[0, rows, :].astype(F32), frag[1, rows, :].astype(F32)
            ).astype(BF16)

        send(sel.at[rows_of((1 - core) * 64, 64), :], got_a, as_sem.at[0], ar_sem.at[0], sib)

    def outer_1():
        arrive(got_a, as_sem.at[0], ar_sem.at[0])

        @pl.loop(0, 4)
        def _(r):
            rows = rows_of(r * 16, 16)
            total = sel[rows_of(row_a + r * 16, 16), :].astype(F32) + got_a[rows, :].astype(F32)
            sum_a[rows, :] = total
            pass_a[rows, :] = total.astype(BF16)

        send(pass_a.at[rows_of((1 - xa) * 32, 32), :], got_b, as_sem.at[1], ar_sem.at[1], near_x)

    def outer_2():
        arrive(got_b, as_sem.at[1], ar_sem.at[1])

        @pl.loop(0, 2)
        def _(r):
            rows = rows_of(r * 16, 16)
            total = sum_a[rows_of(xa * 32 + r * 16, 16), :] + got_b[rows, :].astype(F32)
            sum_b[rows, :] = total
            pass_b[rows, :] = total.astype(BF16)

        send(pass_b.at[rows_of((1 - xb) * 16, 16), :], got_c, as_sem.at[2], ar_sem.at[2], far_x)

    def outer_3():
        arrive(got_c, as_sem.at[2], ar_sem.at[2])
        total = sum_b[rows_of(xb * 16, 16), :] + got_c[...].astype(F32)
        sum_c[...] = total
        pass_c[...] = total.astype(BF16)
        send(
            pass_c.at[:, pl.ds(aligned(1 - yh, HALF), HALF)],
            got_d,
            as_sem.at[3],
            ar_sem.at[3],
            far_y,
        )

    def outer_4():
        arrive(got_d, as_sem.at[3], ar_sem.at[3])
        cols = pl.ds(aligned(yh, HALF), HALF)
        rows = rows_of(row_c, 16)
        drift[rows, cols] = (sum_c[:, cols] + got_d[...].astype(F32)).astype(BF16)
        ref = drift.at[rows, cols]
        send(ref, ref, as_sem.at[4], ar_sem.at[4], far_y)

    def outer_5():
        rows = rows_of(row_c, 16)
        arrive(drift.at[rows, pl.ds(aligned(1 - yh, HALF), HALF)], as_sem.at[4], ar_sem.at[4])
        send(drift.at[rows, :], drift.at[rows, :], as_sem.at[5], ar_sem.at[5], far_x)

    def outer_6():
        arrive(drift.at[rows_of(row_b + (1 - xb) * 16, 16), :], as_sem.at[5], ar_sem.at[5])
        rows = rows_of(row_b, 32)
        send(drift.at[rows, :], drift.at[rows, :], as_sem.at[6], ar_sem.at[6], near_x)

    def outer_7():
        arrive(drift.at[rows_of(row_a + (1 - xa) * 32, 32), :], as_sem.at[6], ar_sem.at[6])
        rows = rows_of(row_a, 64)
        send(drift.at[rows, :], drift.at[rows, :], as_sem.at[7], ar_sem.at[7], sib)

    out_drift = pltpu.make_async_copy(drift, drift_hbm, out_sem.at[0])

    def outer_8():
        arrive(drift.at[rows_of((1 - core) * 64, 64), :], as_sem.at[7], ar_sem.at[7])
        out_drift.start()

    outer_0()

    def chunk_at(offset):
        return lax.rem(z + NZ + offset, NZ)

    def project(chunk, tokens, first=False):
        rows = pl.ds(aligned(chunk, CHUNK), CHUNK)

        @pl.loop(0, 4)
        def _(n):
            cols = pl.ds(aligned(n, 256), 256)
            part = jnp.dot(ctx[tokens, rows], wbuf[rows, cols], preferred_element_type=F32)
            if first:
                proj[tokens, cols] = part
            else:
                proj[tokens, cols] += part

    def turn(tokens):
        @pl.loop(0, NZ)
        def _(n):
            cols = pl.ds(aligned(n, CHUNK), CHUNK)
            ctxt[cols, tokens] = ctx[tokens, cols].T

    own_tok, par_tok = pl.ds(0, TOK), pl.ds(TOK, TOK)
    loc_w.wait()
    loc_ctx.wait()
    project(z, own_tok, first=True)
    turn(own_tok)

    stages = (outer_1, outer_2, outer_3)
    for hop in range(1, 4):
        froms = (chunk_at(-hop), chunk_at(hop))
        for u in range(4):
            for way in range(2):
                arrive(
                    wbuf.at[unit_rows(froms[way], u), :],
                    zs_sem.at[way, hop - 1, u],
                    zr_sem.at[way, hop - 1, u],
                )
                pass_on(hop, u, way, froms[way])
        for way in range(2):
            project(froms[way], own_tok)
        stages[hop - 1]()

    arrive(ctx.at[par_tok, :], ys_sem.at[2], yr_sem.at[2])
    project(z, par_tok, first=True)

    @pl.loop(1, 4)
    def _(hop):
        project(lax.rem(z + hop, NZ), par_tok)
        project(lax.rem(z + NZ - hop, NZ), par_tok)

    turn(par_tok)
    loc_cot.wait()
    arrive(cot.at[par_tok, :], ys_sem.at[3], yr_sem.at[3])
    last = chunk_at(4)
    for u in range(4):
        arrive(wbuf.at[unit_rows(last, u), :], zs_sem.at[u % 2, 3, u], zr_sem.at[u % 2, 3, u])
    project(last, pl.ds(0, PAIR))

    gain = gain_ref[:, pl.ds(mine, HALF)]
    lane = lax.broadcasted_iota(jnp.int32, (UNIT, 128), 1)

    @pl.loop(0, PAIR // UNIT)
    def _(r):
        rows = rows_of(r * UNIT, UNIT)
        p = proj[rows, :]
        scaled = cot[rows, :].astype(F32) * gain
        square = jnp.sum(p * p, axis=1, keepdims=True)
        cross = jnp.sum(scaled * p, axis=1, keepdims=True)
        stat_own[rows, :] = jnp.where(lane == 0, square, jnp.where(lane == 1, cross, 0.0))

    turned = stat_own[...].T[0:8, :]
    stat_send[:, 0:TOK] = turned[:, TOK:PAIR]
    stat_send[:, TOK:PAIR] = turned[:, 0:TOK]
    send(stat_send, stat_recv.at[pl.ds(0, 8), :], ys_sem.at[4], yr_sem.at[4], pair)
    stat_recv[8:128, :] = jnp.zeros((120, PAIR), F32)
    arrive(stat_recv.at[pl.ds(0, 8), :], ys_sem.at[4], yr_sem.at[4])
    stat_own[...] += stat_recv[...].T

    @pl.loop(0, PAIR // UNIT)
    def _(r):
        rows = rows_of(r * UNIT, UNIT)
        stat = stat_own[rows, :] * (1.0 / D)
        inv = lax.rsqrt(stat[:, 0:1] + 1e-06)
        slope = inv * inv * stat[:, 1:2]
        scaled = cot[rows, :].astype(F32) * gain
        pg[rows, :] = (inv * (scaled - proj[rows, :] * slope)).astype(BF16)

    def grad_of(chunk, dst):
        rows = pl.ds(aligned(chunk, CHUNK), CHUNK)

        @pl.loop(0, 4)
        def _(n):
            cols = pl.ds(aligned(n, 256), 256)
            dst[:, cols] = jnp.dot(ctxt[rows, :], pg[:, cols], preferred_element_type=F32)

    def piece_rows(piece, size, offset=0):
        owner = other if piece == 0 else y
        return pl.ds(pl.multiple_of(owner * ROWS + offset, size), size)

    grad_of(chunk_at(4), far)
    for piece in range(2):
        for way in range(2):
            half_send[way, piece] = far[
                piece_rows(piece, ROWS), way * 512 : way * 512 + 512
            ].astype(BF16)
            send(
                half_send.at[way, piece],
                half_recv.at[way, piece],
                hs_sem.at[way, piece],
                hr_sem.at[way, piece],
                ring[way],
            )

    def back(tokens, cols):
        return lax.dot_general(
            pg[tokens, :], wbuf[cols, :], (((1,), (1,)), ((), ())), preferred_element_type=F32
        )

    for q in range(4):
        @pl.loop(0, 2)
        def _(n):
            cols = pl.ds(pl.multiple_of(q * 512 + n * 256, 256), 256)
            cg_send[:, cols] = back(par_tok, cols).astype(BF16)

        cols = pl.ds(q * 512, 512)
        send(cg_send.at[:, cols], cg_recv.at[:, cols], ys_sem.at[5 + q], yr_sem.at[5 + q], pair)

    for way in range(2):
        grad_of(chunk_at(3 if way == 0 else -3), parts.at[way, 0])

    def forward(hop, piece, t, way):
        n = 2 * piece + t
        rows = pl.ds(t * UNIT, UNIT)
        src = parts.at[way, 3 - hop]
        own = src[piece_rows(piece, UNIT, t * UNIT), :]
        if hop == 3:
            if t == 0:
                arrive(
                    half_recv.at[way, piece], hs_sem.at[way, piece], hr_sem.at[way, piece]
                )
            cut = slice(way * 512, way * 512 + 512)
            rest = slice(512 - way * 512, 1024 - way * 512)
            full_send[way, 0, n, :, cut] = (
                own[:, cut] + half_recv[way, piece, rows, :].astype(F32)
            ).astype(BF16)
            full_send[way, 0, n, :, rest] = own[:, rest].astype(BF16)
        else:
            arrive(
                full_recv.at[way, 2 - hop, n], fs_sem.at[way, 2 - hop, n], fr_sem.at[way, 2 - hop, n]
            )
            full_send[way, 3 - hop, n] = (
                own + full_recv[way, 2 - hop, n].astype(F32)
            ).astype(BF16)
        send(
            full_send.at[way, 3 - hop, n],
            full_recv.at[way, 3 - hop, n],
            fs_sem.at[way, 3 - hop, n],
            fr_sem.at[way, 3 - hop, n],
            ring[way],
        )

    def own_back():
        @pl.loop(0, NZ)
        def _(n):
            cols = pl.ds(aligned(n, 256), 256)
            cg_own[:, cols] = back(own_tok, cols)

    out_cg = pltpu.make_async_copy(cg_out, cg_hbm, out_sem.at[1])

    def finish_back():
        for q in range(4):
            cols = pl.ds(q * 512, 512)
            arrive(cg_recv.at[:, cols], ys_sem.at[5 + q], yr_sem.at[5 + q])

        @pl.loop(0, 16)
        def _(r):
            rows = rows_of(r * 16, 16)
            cg_out[rows, :] = (cg_own[rows, :] + cg_recv[rows, :].astype(F32)).astype(BF16)

        out_cg.start()

    def hop_of(hop, between):
        for piece in range(2):
            for t in range(2):
                for way in range(2):
                    forward(hop, piece, t, way)
            between[piece]()

    def next_parts(hop):
        for way in range(2):
            grad_of(chunk_at(hop if way == 0 else -hop), parts.at[way, 3 - hop])

    def after_3a():
        next_parts(2)
        outer_4()

    def after_3b():
        own_back()
        outer_5()

    def after_2a():
        next_parts(1)
        outer_6()

    def after_2b():
        grad_of(z, far)
        outer_7()

    hop_of(3, (after_3a, after_3b))
    hop_of(2, (after_2a, after_2b))
    hop_of(1, (outer_8, finish_back))

    out_own = pltpu.make_async_copy(
        grad_out.at[0], grad_hbm.at[:, pl.ds(mine, HALF)], out_sem.at[2]
    )
    out_par = pltpu.make_async_copy(
        grad_out.at[1], grad_hbm.at[:, pl.ds(theirs, HALF)], out_sem.at[3]
    )
    for piece in range(2):
        for t in range(2):
            n = 2 * piece + t
            rows = pl.ds(t * UNIT, UNIT)
            total = far[piece_rows(piece, UNIT, t * UNIT), :]
            for way in range(2):
                arrive(full_recv.at[way, 2, n], fs_sem.at[way, 2, n], fr_sem.at[way, 2, n])
                total = total + full_recv[way, 2, n].astype(F32)
            if piece == 0:
                y_send[t] = total.astype(BF16)
                send(y_send.at[t], y_recv.at[t], ys_sem.at[9 + t], yr_sem.at[9 + t], pair)
            else:
                grad_out[0, rows, :] = total
    out_own.start()
    for t in range(2):
        arrive(y_recv.at[t], ys_sem.at[9 + t], yr_sem.at[9 + t])
        grad_out[1, t * UNIT : (t + 1) * UNIT, :] = y_recv[t].astype(F32)
    out_par.start()
    for copy in sends:
        copy.wait_send()
    for copy in (out_drift, out_cg, out_own, out_par):
        copy.wait()


def exchange(context, cotangent, gain, weight, frags, step):
    anywhere = pl.BlockSpec(memory_space=pl.ANY)
    dma = pltpu.SemaphoreType.DMA
    return pl.pallas_call(
        kernel,
        out_shape=(
            jax.ShapeDtypeStruct((TOK, D), BF16),
            jax.ShapeDtypeStruct((ROWS, D), F32),
            jax.ShapeDtypeStruct((ROWS, D), BF16),
        ),
        in_specs=[
            anywhere,
            anywhere,
            pl.BlockSpec(memory_space=pltpu.VMEM),
            anywhere,
            anywhere,
            pl.BlockSpec(memory_space=pltpu.SMEM),
        ],
        out_specs=(anywhere, anywhere, anywhere),
        scratch_shapes=[
            pltpu.VMEM((D, HALF), BF16),
            pltpu.VMEM((PAIR, D), BF16),
            pltpu.VMEM((PAIR, HALF), BF16),
            pltpu.VMEM((PAIR, HALF), F32),
            pltpu.VMEM((PAIR, HALF), BF16),
            pltpu.VMEM((D, PAIR), BF16),
            pltpu.VMEM((PAIR, 128), F32),
            pltpu.VMEM((8, PAIR), F32),
            pltpu.VMEM((128, PAIR), F32),
            pltpu.VMEM((CHUNK, HALF), F32),
            pltpu.VMEM((2, 3, CHUNK, HALF), F32),
            pltpu.VMEM((2, 2, ROWS, 512), BF16),
            pltpu.VMEM((2, 2, ROWS, 512), BF16),
            pltpu.VMEM((2, 3, 4, UNIT, HALF), BF16),
            pltpu.VMEM((2, 3, 4, UNIT, HALF), BF16),
            pltpu.VMEM((2, UNIT, HALF), BF16),
            pltpu.VMEM((2, UNIT, HALF), BF16),
            pltpu.VMEM((2, ROWS, HALF), F32),
            pltpu.VMEM((TOK, D), F32),
            pltpu.VMEM((TOK, D), BF16),
            pltpu.VMEM((TOK, D), BF16),
            pltpu.VMEM((TOK, D), BF16),
            pltpu.VMEM((NFRAG, ROWS, D), BF16),
            pltpu.VMEM((ROWS, D), BF16),
            pltpu.VMEM((64, D), F32),
            pltpu.VMEM((32, D), F32),
            pltpu.VMEM((16, D), F32),
            pltpu.VMEM((64, D), BF16),
            pltpu.VMEM((32, D), BF16),
            pltpu.VMEM((16, D), BF16),
            pltpu.VMEM((64, D), BF16),
            pltpu.VMEM((32, D), BF16),
            pltpu.VMEM((16, D), BF16),
            pltpu.VMEM((16, HALF), BF16),
            pltpu.VMEM((ROWS, D), BF16),
            dma((4,)),
            dma((4,)),
            dma((2, 4, 4)),
            dma((2, 4, 4)),
            dma((11,)),
            dma((11,)),
            dma((2, 2)),
            dma((2, 2)),
            dma((2, 3, 4)),
            dma((2, 3, 4)),
            dma((8,)),
            dma((8,)),
        ],
        compiler_params=pltpu.CompilerParams(
            collective_id=0, has_side_effects=True, vmem_limit_bytes=46 * 2**20
        ),
        cost_estimate=pl.CostEstimate(
            flops=6 * TOK * D * D, bytes_accessed=8 * 2**20, transcendentals=PAIR
        ),
        name="exchange",
    )(context, cotangent, gain, weight, frags, step)


def local(
    context,
    cotangent,
    norm_gain,
    out_weight,
    moment_one,
    moment_two,
    local_frags,
    anchors,
    outer_moment,
    outer_step,
):
    ctx_grad, weight_grad, drift = exchange(
        context, cotangent, norm_gain.reshape(1, D), out_weight, local_frags, outer_step
    )
    first_new = beta_one * moment_one[0] + (1.0 - beta_one) * weight_grad
    second_new = beta_two * moment_two[0] + (1.0 - beta_two) * weight_grad * weight_grad
    weight_f = out_weight[0].astype(F32)
    update = first_new / (jnp.sqrt(second_new) + adam_eps) + decay_rate * weight_f
    new_weight = (weight_f - inner_rate * update).astype(BF16)
    due_index = outer_step[0] % NFRAG
    step_rate = rate_base + rate_base * jnp.minimum(outer_step[0], 1000).astype(F32) / 1000.0
    anchor_due = lax.dynamic_index_in_dim(anchors, due_index, 0, keepdims=False).astype(F32)
    moment_due = lax.dynamic_index_in_dim(outer_moment, due_index, 0, keepdims=False)
    islands = lax.axis_size("island")
    pseudo = anchor_due - drift.astype(F32) / islands
    moment_new = outer_mu * moment_due + pseudo
    anchor_new = (anchor_due - step_rate * (pseudo + outer_mu * moment_new)).astype(BF16)
    return (ctx_grad, new_weight[None], first_new[None], second_new[None], anchor_new, moment_new)


def solution(mesh):
    return jax.shard_map(
        local,
        mesh=mesh,
        in_specs=(
            P(("island", "fsdp"), None),
            P(("island", "fsdp"), None),
            P(),
            P("island", "fsdp", None),
            P("island", "fsdp", None),
            P("island", "fsdp", None),
            P("island", None, "fsdp", None),
            P(None, "fsdp", None),
            P(None, "fsdp", None),
            P(),
        ),
        out_specs=(
            P(("island", "fsdp"), None),
            P("island", "fsdp", None),
            P("island", "fsdp", None),
            P("island", "fsdp", None),
            P("fsdp", None),
            P("fsdp", None),
        ),
        check_vma=False,
    )
```

```python
import functools

import jax
import jax.numpy as jnp
from jax import lax
from jax.experimental import pallas as pl
from jax.experimental.pallas import tpu as pltpu
from jax.sharding import PartitionSpec as P

NFRAG = 2
N_ISLAND = 16

beta_one = 0.9
beta_two = 0.95
inner_rate = 0.01
decay_rate = 0.1
adam_eps = 1e-08
outer_mu = 0.9
rate_base = 0.35

NZ = 8
TOK = 256
PAIR = 512
D = 2048
HALF = 1024
ROWS = 128
CHUNK = 256
UNIT = 64

F32 = jnp.float32
BF16 = jnp.bfloat16
MESH = pl.DeviceIdType.MESH


def aligned(value, size):
    return pl.multiple_of(value * size, size)


def kernel(
    ctx_hbm,
    cot_hbm,
    gain_hbm,
    w_hbm,
    frag_hbm,
    step_ref,
    cg_hbm,
    grad_hbm,
    drift_hbm,
    wbuf,
    ctx,
    cot,
    gain_buf,
    proj,
    pg,
    ctxt,
    stat_own,
    stat_send,
    stat_recv,
    far,
    parts,
    half_send,
    half_recv,
    full_send,
    full_recv,
    y_send,
    y_recv,
    grad_out,
    cg_own,
    cg_send,
    cg_recv,
    cg_out,
    frag,
    sel,
    sum_a,
    sum_b,
    sum_c,
    pass_a,
    pass_b,
    pass_c,
    got_a,
    got_b,
    got_c,
    got_d,
    drift,
    loc_sem,
    out_sem,
    zs_sem,
    zr_sem,
    ys_sem,
    yr_sem,
    hs_sem,
    hr_sem,
    fs_sem,
    fr_sem,
    as_sem,
    ar_sem,
):
    isl = lax.axis_index("island")
    fsd = lax.axis_index("fsdp")
    y = lax.rem(fsd, 2)
    z = lax.div(fsd, 2)
    core = lax.rem(isl, 2)
    x = lax.rem(lax.div(isl, 2), 4)
    yh = lax.div(isl, 8)
    xa = lax.rem(x, 2)
    xb = lax.div(x, 2)
    other = 1 - y
    up = (isl, lax.rem(z + 1, NZ) * 2 + y)
    down = (isl, lax.rem(z + NZ - 1, NZ) * 2 + y)
    ring = (up, down)
    pair = (isl, z * 2 + other)
    sib = (isl + 1 - 2 * core, fsd)
    near_x = (isl + 2 - 4 * xa, fsd)
    far_x = (isl + 4 - 8 * xb, fsd)
    far_y = (isl + 8 - 16 * yh, fsd)
    mine = aligned(y, HALF)
    theirs = aligned(other, HALF)

    sends = []

    def send(src, dst, ss, rs, dev):
        copy = pltpu.make_async_remote_copy(
            src_ref=src, dst_ref=dst, send_sem=ss, recv_sem=rs, device_id=dev, device_id_type=MESH
        )
        copy.start()
        sends.append(copy)

    def arrive(dst, ss, rs):
        pltpu.make_async_remote_copy(
            src_ref=dst, dst_ref=dst, send_sem=ss, recv_sem=rs, device_id=pair, device_id_type=MESH
        ).wait_recv()

    loc_w = pltpu.make_async_copy(
        w_hbm.at[0, :, pl.ds(mine, HALF)], wbuf.at[pl.ds(aligned(fsd, ROWS), ROWS), :], loc_sem.at[0]
    )
    loc_ctx = pltpu.make_async_copy(ctx_hbm, ctx.at[pl.ds(0, TOK), :], loc_sem.at[1])
    loc_cot = pltpu.make_async_copy(
        cot_hbm.at[:, pl.ds(mine, HALF)], cot.at[pl.ds(0, TOK), :], loc_sem.at[2]
    )
    loc_frag = pltpu.make_async_copy(frag_hbm.at[0], frag, loc_sem.at[3])
    loc_gain = pltpu.make_async_copy(gain_hbm.at[:, pl.ds(mine, HALF)], gain_buf, loc_sem.at[4])
    for copy in (loc_w, loc_frag, loc_ctx, loc_cot, loc_gain):
        copy.start()

    barrier = pltpu.get_barrier_semaphore()
    for dev in (up, down, pair, sib, near_x, far_x, far_y):
        pl.semaphore_signal(barrier, inc=1, device_id=dev, device_id_type=MESH)
    pl.semaphore_wait(barrier, 7)

    def unit_rows(z_from, u):
        owner = y if u < 2 else other
        return pl.ds(pl.multiple_of(z_from * CHUNK + owner * ROWS + (u % 2) * UNIT, UNIT), UNIT)

    for t in range(2):
        rows = pl.ds(t * UNIT, UNIT)
        send(
            w_hbm.at[0, rows, pl.ds(theirs, HALF)],
            wbuf.at[unit_rows(z, t), :],
            ys_sem.at[t],
            yr_sem.at[t],
            pair,
        )
        for way in range(2):
            send(
                w_hbm.at[0, rows, pl.ds(mine, HALF)],
                wbuf.at[unit_rows(z, t), :],
                zs_sem.at[way, 0, t],
                zr_sem.at[way, 0, t],
                ring[way],
            )

    def pass_on(hop, u, way, z_from):
        if hop < 3 or (u % 2) == way:
            ref = wbuf.at[unit_rows(z_from, u), :]
            send(ref, ref, zs_sem.at[way, hop, u], zr_sem.at[way, hop, u], ring[way])

    for t in range(2):
        arrive(wbuf.at[unit_rows(z, 2 + t), :], ys_sem.at[t], yr_sem.at[t])
        for way in range(2):
            pass_on(0, 2 + t, way, z)

    send(ctx_hbm, ctx.at[pl.ds(TOK, TOK), :], ys_sem.at[2], yr_sem.at[2], pair)
    send(
        cot_hbm.at[:, pl.ds(theirs, HALF)],
        cot.at[pl.ds(TOK, TOK), :],
        ys_sem.at[3],
        yr_sem.at[3],
        pair,
    )

    row_a = core * 64
    row_b = row_a + xa * 32
    row_c = row_b + xb * 16

    def rows_of(start, size):
        return pl.ds(pl.multiple_of(start, size), size)

    def outer_0():
        loc_frag.wait()
        due = jnp.full((16, D), jnp.bitwise_and(step_ref[0], 1), jnp.int32)

        @pl.loop(0, 8)
        def _(r):
            rows = rows_of(r * 16, 16)
            sel[rows, :] = jnp.where(
                due == 0, frag[0, rows, :].astype(F32), frag[1, rows, :].astype(F32)
            ).astype(BF16)

        send(sel.at[rows_of((1 - core) * 64, 64), :], got_a, as_sem.at[0], ar_sem.at[0], sib)

    def outer_1():
        arrive(got_a, as_sem.at[0], ar_sem.at[0])

        @pl.loop(0, 4)
        def _(r):
            rows = rows_of(r * 16, 16)
            total = sel[rows_of(row_a + r * 16, 16), :].astype(F32) + got_a[rows, :].astype(F32)
            sum_a[rows, :] = total
            pass_a[rows, :] = total.astype(BF16)

        send(pass_a.at[rows_of((1 - xa) * 32, 32), :], got_b, as_sem.at[1], ar_sem.at[1], near_x)

    def outer_2():
        arrive(got_b, as_sem.at[1], ar_sem.at[1])

        @pl.loop(0, 2)
        def _(r):
            rows = rows_of(r * 16, 16)
            total = sum_a[rows_of(xa * 32 + r * 16, 16), :] + got_b[rows, :].astype(F32)
            sum_b[rows, :] = total
            pass_b[rows, :] = total.astype(BF16)

        send(pass_b.at[rows_of((1 - xb) * 16, 16), :], got_c, as_sem.at[2], ar_sem.at[2], far_x)

    def outer_3():
        arrive(got_c, as_sem.at[2], ar_sem.at[2])
        total = sum_b[rows_of(xb * 16, 16), :] + got_c[...].astype(F32)
        sum_c[...] = total
        pass_c[...] = total.astype(BF16)
        send(
            pass_c.at[:, pl.ds(aligned(1 - yh, HALF), HALF)],
            got_d,
            as_sem.at[3],
            ar_sem.at[3],
            far_y,
        )

    def outer_4():
        arrive(got_d, as_sem.at[3], ar_sem.at[3])
        cols = pl.ds(aligned(yh, HALF), HALF)
        rows = rows_of(row_c, 16)
        drift[rows, cols] = (sum_c[:, cols] + got_d[...].astype(F32)).astype(BF16)
        ref = drift.at[rows, cols]
        send(ref, ref, as_sem.at[4], ar_sem.at[4], far_y)

    def outer_5():
        rows = rows_of(row_c, 16)
        arrive(drift.at[rows, pl.ds(aligned(1 - yh, HALF), HALF)], as_sem.at[4], ar_sem.at[4])
        send(drift.at[rows, :], drift.at[rows, :], as_sem.at[5], ar_sem.at[5], far_x)

    def outer_6():
        arrive(drift.at[rows_of(row_b + (1 - xb) * 16, 16), :], as_sem.at[5], ar_sem.at[5])
        rows = rows_of(row_b, 32)
        send(drift.at[rows, :], drift.at[rows, :], as_sem.at[6], ar_sem.at[6], near_x)

    def outer_7():
        arrive(drift.at[rows_of(row_a + (1 - xa) * 32, 32), :], as_sem.at[6], ar_sem.at[6])
        rows = rows_of(row_a, 64)
        send(drift.at[rows, :], drift.at[rows, :], as_sem.at[7], ar_sem.at[7], sib)

    out_drift = pltpu.make_async_copy(drift, drift_hbm, out_sem.at[0])

    def outer_8():
        arrive(drift.at[rows_of((1 - core) * 64, 64), :], as_sem.at[7], ar_sem.at[7])
        out_drift.start()

    stat_recv[:, 8:128, :] = jnp.zeros((2, 120, TOK), F32)
    outer_0()

    def chunk_at(offset):
        return lax.rem(z + NZ + offset, NZ)

    def chunk_rows(offset):
        return pl.ds(aligned(chunk_at(offset), CHUNK), CHUNK)

    def project(chunk, tokens, first=False):
        rows = pl.ds(aligned(chunk, CHUNK), CHUNK)

        @pl.loop(0, 4)
        def _(n):
            cols = pl.ds(aligned(n, 256), 256)
            part = jnp.dot(ctx[tokens, rows], wbuf[rows, cols], preferred_element_type=F32)
            if first:
                proj[tokens, cols] = part
            else:
                proj[tokens, cols] += part

    def turn(tokens):
        @pl.loop(0, NZ)
        def _(n):
            cols = pl.ds(aligned(n, CHUNK), CHUNK)
            ctxt[cols, tokens] = ctx[tokens, cols].T

    own_tok, par_tok = pl.ds(0, TOK), pl.ds(TOK, TOK)
    loc_w.wait()
    loc_ctx.wait()
    project(z, own_tok, first=True)
    turn(own_tok)

    stages = (outer_1, outer_2, outer_3)
    for hop in range(1, 4):
        froms = (chunk_at(-hop), chunk_at(hop))
        for u in range(4):
            for way in range(2):
                arrive(
                    wbuf.at[unit_rows(froms[way], u), :],
                    zs_sem.at[way, hop - 1, u],
                    zr_sem.at[way, hop - 1, u],
                )
                pass_on(hop, u, way, froms[way])
            if hop == 3 and u == 2:
                arrive(ctx.at[par_tok, :], ys_sem.at[2], yr_sem.at[2])
                project(z, par_tok, first=True)
                for near in (1, -1, 2, -2):
                    project(chunk_at(near), par_tok)
        for way in range(2):
            project(froms[way], own_tok)
            if hop == 3:
                project(froms[way], par_tok)
        stages[hop - 1]()

    def project_part(owner, tokens):
        rows = pl.ds(pl.multiple_of(chunk_at(4) * CHUNK + owner * ROWS, ROWS), ROWS)

        @pl.loop(0, 4)
        def _(n):
            cols = pl.ds(aligned(n, 256), 256)
            proj[tokens, cols] += jnp.dot(
                ctx[tokens, rows], wbuf[rows, cols], preferred_element_type=F32
            )

    last = chunk_at(4)
    for u in range(4):
        arrive(wbuf.at[unit_rows(last, u), :], zs_sem.at[u % 2, 3, u], zr_sem.at[u % 2, 3, u])
        if u == 1:
            project_part(y, pl.ds(0, PAIR))
            loc_cot.wait()
            loc_gain.wait()
            arrive(cot.at[par_tok, :], ys_sem.at[3], yr_sem.at[3])

    gain = gain_buf[...]
    lane = lax.broadcasted_iota(jnp.int32, (UNIT, 128), 1)

    def stat_sem(half):
        return 4 if half == 1 else 11

    for half in (1, 0):
        project_part(other, pl.ds(half * TOK, TOK))

        @pl.loop(0, TOK // UNIT)
        def _(r):
            rows = rows_of(half * TOK + r * UNIT, UNIT)
            p = proj[rows, :]
            scaled = cot[rows, :].astype(F32) * gain
            square = jnp.sum(p * p, axis=1, keepdims=True)
            cross = jnp.sum(scaled * p, axis=1, keepdims=True)
            stat_own[rows, :] = jnp.where(lane == 0, square, jnp.where(lane == 1, cross, 0.0))

        stat_send[half] = stat_own[half * TOK : half * TOK + TOK, :].T[0:8, :]
        k = stat_sem(half)
        send(
            stat_send.at[half],
            stat_recv.at[1 - half, pl.ds(0, 8), :],
            ys_sem.at[k],
            yr_sem.at[k],
            pair,
        )

    turn(par_tok)
    for half in range(2):
        k = stat_sem(1 - half)
        arrive(stat_recv.at[half, pl.ds(0, 8), :], ys_sem.at[k], yr_sem.at[k])
        stat_own[half * TOK : half * TOK + TOK, :] += stat_recv[half].T

        @pl.loop(0, TOK // UNIT)
        def _(r):
            rows = rows_of(half * TOK + r * UNIT, UNIT)
            stat = stat_own[rows, :] * (1.0 / D)
            inv = lax.rsqrt(stat[:, 0:1] + 1e-06)
            slope = inv * inv * stat[:, 1:2]
            scaled = cot[rows, :].astype(F32) * gain
            pg[rows, :] = (inv * (scaled - proj[rows, :] * slope)).astype(BF16)

    def grad_of(rows, dst):
        @pl.loop(0, 4)
        def _(n):
            cols = pl.ds(aligned(n, 256), 256)
            dst[:, cols] = jnp.dot(ctxt[rows, :], pg[:, cols], preferred_element_type=F32)

    def piece_rows(piece, size, offset=0):
        owner = other if piece == 0 else y
        return pl.ds(pl.multiple_of(owner * ROWS + offset, size), size)

    for piece in range(2):
        owner = other if piece == 0 else y
        rows = pl.ds(pl.multiple_of(chunk_at(4) * CHUNK + owner * ROWS, ROWS), ROWS)
        grad_of(rows, far.at[piece_rows(piece, ROWS), :])
        for way in range(2):
            half_send[way, piece] = far[
                piece_rows(piece, ROWS), way * 512 : way * 512 + 512
            ].astype(BF16)
            send(
                half_send.at[way, piece],
                half_recv.at[way, piece],
                hs_sem.at[way, piece],
                hr_sem.at[way, piece],
                ring[way],
            )

    def back(tokens, cols):
        return lax.dot_general(
            pg[tokens, :], wbuf[cols, :], (((1,), (1,)), ((), ())), preferred_element_type=F32
        )

    for q in range(4):
        @pl.loop(0, 2)
        def _(n):
            cols = pl.ds(pl.multiple_of(q * 512 + n * 256, 256), 256)
            cg_send[:, cols] = back(par_tok, cols).astype(BF16)

        cols = pl.ds(q * 512, 512)
        send(cg_send.at[:, cols], cg_recv.at[:, cols], ys_sem.at[5 + q], yr_sem.at[5 + q], pair)

    for way in range(2):
        grad_of(chunk_rows(3 if way == 0 else -3), parts.at[way, 0])

    def forward(hop, piece, t, way):
        n = 2 * piece + t
        rows = pl.ds(t * UNIT, UNIT)
        src = parts.at[way, 3 - hop]
        own = src[piece_rows(piece, UNIT, t * UNIT), :]
        if hop == 3:
            if t == 0:
                arrive(
                    half_recv.at[way, piece], hs_sem.at[way, piece], hr_sem.at[way, piece]
                )
            cut = slice(way * 512, way * 512 + 512)
            rest = slice(512 - way * 512, 1024 - way * 512)
            full_send[way, 0, n, :, cut] = (
                own[:, cut] + half_recv[way, piece, rows, :].astype(F32)
            ).astype(BF16)
            full_send[way, 0, n, :, rest] = own[:, rest].astype(BF16)
        else:
            arrive(
                full_recv.at[way, 2 - hop, n], fs_sem.at[way, 2 - hop, n], fr_sem.at[way, 2 - hop, n]
            )
            full_send[way, 3 - hop, n] = (
                own + full_recv[way, 2 - hop, n].astype(F32)
            ).astype(BF16)
        send(
            full_send.at[way, 3 - hop, n],
            full_recv.at[way, 3 - hop, n],
            fs_sem.at[way, 3 - hop, n],
            fr_sem.at[way, 3 - hop, n],
            ring[way],
        )

    def own_back():
        @pl.loop(0, NZ)
        def _(n):
            cols = pl.ds(aligned(n, 256), 256)
            cg_own[:, cols] = back(own_tok, cols)

    out_cg = pltpu.make_async_copy(cg_out, cg_hbm, out_sem.at[1])

    def finish_back():
        for q in range(4):
            cols = pl.ds(q * 512, 512)
            arrive(cg_recv.at[:, cols], ys_sem.at[5 + q], yr_sem.at[5 + q])

        @pl.loop(0, 16)
        def _(r):
            rows = rows_of(r * 16, 16)
            cg_out[rows, :] = (cg_own[rows, :] + cg_recv[rows, :].astype(F32)).astype(BF16)

        out_cg.start()

    def hop_of(hop, between):
        for piece in range(2):
            for t in range(2):
                for way in range(2):
                    forward(hop, piece, t, way)
            between[piece]()

    def next_parts(hop):
        for way in range(2):
            grad_of(chunk_rows(hop if way == 0 else -hop), parts.at[way, 3 - hop])

    def after_3a():
        next_parts(2)
        outer_4()

    def after_3b():
        own_back()
        outer_5()

    def after_2a():
        next_parts(1)
        outer_6()

    def after_2b():
        grad_of(chunk_rows(0), far)
        outer_7()

    hop_of(3, (after_3a, after_3b))
    hop_of(2, (after_2a, after_2b))
    hop_of(1, (outer_8, finish_back))

    out_own = pltpu.make_async_copy(
        grad_out.at[0], grad_hbm.at[:, pl.ds(mine, HALF)], out_sem.at[2]
    )
    out_par = pltpu.make_async_copy(
        grad_out.at[1], grad_hbm.at[:, pl.ds(theirs, HALF)], out_sem.at[3]
    )
    for piece in range(2):
        for t in range(2):
            n = 2 * piece + t
            rows = pl.ds(t * UNIT, UNIT)
            total = far[piece_rows(piece, UNIT, t * UNIT), :]
            for way in range(2):
                arrive(full_recv.at[way, 2, n], fs_sem.at[way, 2, n], fr_sem.at[way, 2, n])
                total = total + full_recv[way, 2, n].astype(F32)
            if piece == 0:
                y_send[t] = total.astype(BF16)
                send(y_send.at[t], y_recv.at[t], ys_sem.at[9 + t], yr_sem.at[9 + t], pair)
            else:
                grad_out[0, rows, :] = total
    out_own.start()
    for t in range(2):
        arrive(y_recv.at[t], ys_sem.at[9 + t], yr_sem.at[9 + t])
        grad_out[1, t * UNIT : (t + 1) * UNIT, :] = y_recv[t].astype(F32)
    out_par.start()
    for copy in sends:
        copy.wait_send()
    for copy in (out_drift, out_cg, out_own, out_par):
        copy.wait()


def exchange(context, cotangent, gain, weight, frags, step):
    anywhere = pl.BlockSpec(memory_space=pl.ANY)
    in_hbm = pl.BlockSpec(memory_space=pltpu.HBM)
    dma = pltpu.SemaphoreType.DMA
    return pl.pallas_call(
        kernel,
        out_shape=(
            jax.ShapeDtypeStruct((TOK, D), BF16),
            jax.ShapeDtypeStruct((ROWS, D), F32),
            jax.ShapeDtypeStruct((ROWS, D), BF16),
        ),
        in_specs=[
            in_hbm,
            in_hbm,
            in_hbm,
            in_hbm,
            in_hbm,
            pl.BlockSpec(memory_space=pltpu.SMEM),
        ],
        out_specs=(anywhere, anywhere, anywhere),
        scratch_shapes=[
            pltpu.VMEM((D, HALF), BF16),
            pltpu.VMEM((PAIR, D), BF16),
            pltpu.VMEM((PAIR, HALF), BF16),
            pltpu.VMEM((1, HALF), F32),
            pltpu.VMEM((PAIR, HALF), F32),
            pltpu.VMEM((PAIR, HALF), BF16),
            pltpu.VMEM((D, PAIR), BF16),
            pltpu.VMEM((PAIR, 128), F32),
            pltpu.VMEM((2, 8, TOK), F32),
            pltpu.VMEM((2, 128, TOK), F32),
            pltpu.VMEM((CHUNK, HALF), F32),
            pltpu.VMEM((2, 3, CHUNK, HALF), F32),
            pltpu.VMEM((2, 2, ROWS, 512), BF16),
            pltpu.VMEM((2, 2, ROWS, 512), BF16),
            pltpu.VMEM((2, 3, 4, UNIT, HALF), BF16),
            pltpu.VMEM((2, 3, 4, UNIT, HALF), BF16),
            pltpu.VMEM((2, UNIT, HALF), BF16),
            pltpu.VMEM((2, UNIT, HALF), BF16),
            pltpu.VMEM((2, ROWS, HALF), F32),
            pltpu.VMEM((TOK, D), F32),
            pltpu.VMEM((TOK, D), BF16),
            pltpu.VMEM((TOK, D), BF16),
            pltpu.VMEM((TOK, D), BF16),
            pltpu.VMEM((NFRAG, ROWS, D), BF16),
            pltpu.VMEM((ROWS, D), BF16),
            pltpu.VMEM((64, D), F32),
            pltpu.VMEM((32, D), F32),
            pltpu.VMEM((16, D), F32),
            pltpu.VMEM((64, D), BF16),
            pltpu.VMEM((32, D), BF16),
            pltpu.VMEM((16, D), BF16),
            pltpu.VMEM((64, D), BF16),
            pltpu.VMEM((32, D), BF16),
            pltpu.VMEM((16, D), BF16),
            pltpu.VMEM((16, HALF), BF16),
            pltpu.VMEM((ROWS, D), BF16),
            dma((5,)),
            dma((4,)),
            dma((2, 4, 4)),
            dma((2, 4, 4)),
            dma((12,)),
            dma((12,)),
            dma((2, 2)),
            dma((2, 2)),
            dma((2, 3, 4)),
            dma((2, 3, 4)),
            dma((8,)),
            dma((8,)),
        ],
        compiler_params=pltpu.CompilerParams(
            collective_id=0, has_side_effects=True, vmem_limit_bytes=46 * 2**20
        ),
        cost_estimate=pl.CostEstimate(
            flops=6 * TOK * D * D, bytes_accessed=8 * 2**20, transcendentals=PAIR
        ),
        name="exchange",
    )(*(pltpu.with_memory_space_constraint(a, pltpu.HBM) for a in (context, cotangent, gain, weight, frags)), step)


def finish_kernel(
    step_ref,
    cg_ref,
    grad_ref,
    drift_ref,
    one_ref,
    two_ref,
    weight_ref,
    anchors_ref,
    momenta_ref,
    cg_hbm,
    weight_hbm,
    one_hbm,
    two_hbm,
    anchor_hbm,
    momentum_hbm,
    weight_buf,
    one_buf,
    two_buf,
    anchor_buf,
    momentum_buf,
    sem,
):
    copies = []

    def put(src, dst):
        copy = pltpu.make_async_copy(src, dst, sem.at[len(copies)])
        copy.start()
        copies.append(copy)

    put(cg_ref, cg_hbm)
    step = step_ref[0]
    due = lax.rem(step, NFRAG)
    rate = rate_base + rate_base * jnp.minimum(step, 1000).astype(F32) / 1000.0
    for block in range(4):
        @pl.loop(0, 2)
        def _(r):
            rows = pl.ds(pl.multiple_of(block * 32 + r * 16, 16), 16)
            first = beta_one * one_ref[0, rows, :] + (1.0 - beta_one) * grad_ref[rows, :]
            grad = grad_ref[rows, :]
            second = beta_two * two_ref[0, rows, :] + (1.0 - beta_two) * grad * grad
            weight = weight_ref[0, rows, :].astype(F32)
            update = first / (jnp.sqrt(second) + adam_eps) + decay_rate * weight
            one_buf[rows, :] = first
            two_buf[rows, :] = second
            weight_buf[rows, :] = (weight - inner_rate * update).astype(BF16)

        rows = pl.ds(block * 32, 32)
        put(one_buf.at[rows, :], one_hbm.at[0, rows, :])
        put(two_buf.at[rows, :], two_hbm.at[0, rows, :])
        put(weight_buf.at[rows, :], weight_hbm.at[0, rows, :])

    for block in range(2):
        @pl.loop(0, 4)
        def _(r):
            rows = pl.ds(pl.multiple_of(block * 64 + r * 16, 16), 16)
            anchor = anchors_ref[due, rows, :].astype(F32)
            pseudo = anchor - drift_ref[rows, :].astype(F32) / N_ISLAND
            momentum = outer_mu * momenta_ref[due, rows, :] + pseudo
            momentum_buf[rows, :] = momentum
            anchor_buf[rows, :] = (anchor - rate * (pseudo + outer_mu * momentum)).astype(BF16)

        rows = pl.ds(block * 64, 64)
        put(momentum_buf.at[rows, :], momentum_hbm.at[rows, :])
        put(anchor_buf.at[rows, :], anchor_hbm.at[rows, :])
    for copy in copies:
        copy.wait()


def finish(step, *operands):
    inside = pl.BlockSpec(memory_space=pltpu.VMEM)
    anywhere = pl.BlockSpec(memory_space=pl.ANY)
    return pl.pallas_call(
        finish_kernel,
        out_shape=(
            jax.ShapeDtypeStruct((TOK, D), BF16),
            jax.ShapeDtypeStruct((1, ROWS, D), BF16),
            jax.ShapeDtypeStruct((1, ROWS, D), F32),
            jax.ShapeDtypeStruct((1, ROWS, D), F32),
            jax.ShapeDtypeStruct((ROWS, D), BF16),
            jax.ShapeDtypeStruct((ROWS, D), F32),
        ),
        in_specs=[pl.BlockSpec(memory_space=pltpu.SMEM)] + [inside] * 8,
        out_specs=(anywhere,) * 6,
        scratch_shapes=[
            pltpu.VMEM((ROWS, D), BF16),
            pltpu.VMEM((ROWS, D), F32),
            pltpu.VMEM((ROWS, D), F32),
            pltpu.VMEM((ROWS, D), BF16),
            pltpu.VMEM((ROWS, D), F32),
            pltpu.SemaphoreType.DMA((17,)),
        ],
        compiler_params=pltpu.CompilerParams(vmem_limit_bytes=16 * 2**20),
        cost_estimate=pl.CostEstimate(
            flops=30 * ROWS * D, bytes_accessed=12 * 2**20, transcendentals=ROWS * D
        ),
        name="finish",
    )(step, *operands)


def local(
    context,
    cotangent,
    norm_gain,
    out_weight,
    moment_one,
    moment_two,
    local_frags,
    anchors,
    outer_moment,
    outer_step,
):
    ctx_grad, weight_grad, drift = exchange(
        context, cotangent, norm_gain.reshape(1, D), out_weight, local_frags, outer_step
    )
    return finish(
        outer_step,
        ctx_grad,
        weight_grad,
        drift,
        moment_one,
        moment_two,
        out_weight,
        anchors,
        outer_moment,
    )


def solution(mesh):
    return jax.shard_map(
        local,
        mesh=mesh,
        in_specs=(
            P(("island", "fsdp"), None),
            P(("island", "fsdp"), None),
            P(),
            P("island", "fsdp", None),
            P("island", "fsdp", None),
            P("island", "fsdp", None),
            P("island", None, "fsdp", None),
            P(None, "fsdp", None),
            P(None, "fsdp", None),
            P(),
        ),
        out_specs=(
            P(("island", "fsdp"), None),
            P("island", "fsdp", None),
            P("island", "fsdp", None),
            P("island", "fsdp", None),
            P("fsdp", None),
            P("fsdp", None),
        ),
        check_vma=False,
    )
```

```python
import functools

import jax
import jax.numpy as jnp
from jax import lax
from jax.experimental import pallas as pl
from jax.experimental.pallas import tpu as pltpu
from jax.sharding import PartitionSpec as P

NFRAG = 2
N_ISLAND = 16

beta_one = 0.9
beta_two = 0.95
inner_rate = 0.01
decay_rate = 0.1
adam_eps = 1e-08
outer_mu = 0.9
rate_base = 0.35

NZ = 8
TOK = 256
PAIR = 512
D = 2048
HALF = 1024
ROWS = 128
CHUNK = 256
UNIT = 64

F32 = jnp.float32
BF16 = jnp.bfloat16
MESH = pl.DeviceIdType.MESH


def aligned(value, size):
    return pl.multiple_of(value * size, size)


def kernel(
    ctx_hbm,
    cot_hbm,
    gain_hbm,
    w_hbm,
    frag_hbm,
    step_ref,
    cg_hbm,
    grad_hbm,
    drift_hbm,
    wbuf,
    ctx,
    cot,
    gain_buf,
    proj,
    pg,
    ctxt,
    stat_own,
    stat_send,
    stat_recv,
    far,
    parts,
    half_send,
    half_recv,
    full_send,
    full_recv,
    y_send,
    y_recv,
    grad_out,
    cg_own,
    cg_send,
    cg_recv,
    cg_out,
    frag,
    sel,
    sum_a,
    sum_b,
    pass_a,
    pass_b,
    pass_c,
    got_a,
    got_b,
    got_c,
    got_d,
    drift,
    loc_sem,
    out_sem,
    zs_sem,
    zr_sem,
    ys_sem,
    yr_sem,
    hs_sem,
    hr_sem,
    fs_sem,
    fr_sem,
    as_sem,
    ar_sem,
):
    isl = lax.axis_index("island")
    fsd = lax.axis_index("fsdp")
    y = lax.rem(fsd, 2)
    z = lax.div(fsd, 2)
    core = lax.rem(isl, 2)
    x = lax.rem(lax.div(isl, 2), 4)
    yh = lax.div(isl, 8)
    xa = lax.rem(x, 2)
    xb = lax.div(x, 2)
    other = 1 - y
    up = (isl, lax.rem(z + 1, NZ) * 2 + y)
    down = (isl, lax.rem(z + NZ - 1, NZ) * 2 + y)
    ring = (up, down)
    pair = (isl, z * 2 + other)
    sib = (isl + 1 - 2 * core, fsd)
    near_x = (isl + 2 - 4 * xa, fsd)
    far_x = (isl + 4 - 8 * xb, fsd)
    far_y = (isl + 8 - 16 * yh, fsd)
    mine = aligned(y, HALF)
    theirs = aligned(other, HALF)

    sends = []

    def send(src, dst, ss, rs, dev):
        copy = pltpu.make_async_remote_copy(
            src_ref=src, dst_ref=dst, send_sem=ss, recv_sem=rs, device_id=dev, device_id_type=MESH
        )
        copy.start()
        sends.append(copy)

    def arrive(dst, ss, rs):
        pltpu.make_async_remote_copy(
            src_ref=dst, dst_ref=dst, send_sem=ss, recv_sem=rs, device_id=pair, device_id_type=MESH
        ).wait_recv()

    loc_w = pltpu.make_async_copy(
        w_hbm.at[0, :, pl.ds(mine, HALF)], wbuf.at[pl.ds(aligned(fsd, ROWS), ROWS), :], loc_sem.at[0]
    )
    loc_ctx = pltpu.make_async_copy(ctx_hbm, ctx.at[pl.ds(0, TOK), :], loc_sem.at[1])
    loc_cot = pltpu.make_async_copy(
        cot_hbm.at[:, pl.ds(mine, HALF)], cot.at[pl.ds(0, TOK), :], loc_sem.at[2]
    )
    loc_frag = pltpu.make_async_copy(frag_hbm.at[0], frag, loc_sem.at[3])
    loc_gain = pltpu.make_async_copy(gain_hbm.at[:, pl.ds(mine, HALF)], gain_buf, loc_sem.at[4])
    for copy in (loc_w, loc_frag, loc_ctx, loc_cot, loc_gain):
        copy.start()

    barrier = pltpu.get_barrier_semaphore()
    for dev in (up, down, pair, sib, near_x, far_x, far_y):
        pl.semaphore_signal(barrier, inc=1, device_id=dev, device_id_type=MESH)
    pl.semaphore_wait(barrier, 7)

    def unit_rows(z_from, u):
        owner = y if u < 2 else other
        return pl.ds(pl.multiple_of(z_from * CHUNK + owner * ROWS + (u % 2) * UNIT, UNIT), UNIT)

    for t in range(2):
        rows = pl.ds(t * UNIT, UNIT)
        send(
            w_hbm.at[0, rows, pl.ds(theirs, HALF)],
            wbuf.at[unit_rows(z, t), :],
            ys_sem.at[t],
            yr_sem.at[t],
            pair,
        )
        for way in range(2):
            send(
                w_hbm.at[0, rows, pl.ds(mine, HALF)],
                wbuf.at[unit_rows(z, t), :],
                zs_sem.at[way, 0, t],
                zr_sem.at[way, 0, t],
                ring[way],
            )

    def pass_on(hop, u, way, z_from):
        if hop < 3 or (u % 2) == way:
            ref = wbuf.at[unit_rows(z_from, u), :]
            send(ref, ref, zs_sem.at[way, hop, u], zr_sem.at[way, hop, u], ring[way])

    for t in range(2):
        arrive(wbuf.at[unit_rows(z, 2 + t), :], ys_sem.at[t], yr_sem.at[t])
        for way in range(2):
            pass_on(0, 2 + t, way, z)

    send(ctx_hbm, ctx.at[pl.ds(TOK, TOK), :], ys_sem.at[2], yr_sem.at[2], pair)
    send(
        cot_hbm.at[:, pl.ds(theirs, HALF)],
        cot.at[pl.ds(TOK, TOK), :],
        ys_sem.at[3],
        yr_sem.at[3],
        pair,
    )

    row_a = core * 64
    row_b = row_a + xa * 32
    row_c = row_b + xb * 16

    def rows_of(start, size):
        return pl.ds(pl.multiple_of(start, size), size)

    def outer_0():
        loc_frag.wait()
        due = jnp.full((16, D), jnp.bitwise_and(step_ref[0], 1), jnp.int32)

        @pl.loop(0, 8)
        def _(r):
            rows = rows_of(r * 16, 16)
            sel[rows, :] = jnp.where(
                due == 0, frag[0, rows, :].astype(F32), frag[1, rows, :].astype(F32)
            ).astype(BF16)

        send(sel.at[rows_of((1 - core) * 64, 64), :], got_a, as_sem.at[0], ar_sem.at[0], sib)

    def outer_1():
        arrive(got_a, as_sem.at[0], ar_sem.at[0])

        @pl.loop(0, 4)
        def _(r):
            rows = rows_of(r * 16, 16)
            total = sel[rows_of(row_a + r * 16, 16), :].astype(F32) + got_a[rows, :].astype(F32)
            sum_a[rows, :] = total
            pass_a[rows, :] = total.astype(BF16)

        send(pass_a.at[rows_of((1 - xa) * 32, 32), :], got_b, as_sem.at[1], ar_sem.at[1], near_x)

    def outer_2():
        arrive(got_b, as_sem.at[1], ar_sem.at[1])

        @pl.loop(0, 2)
        def _(r):
            rows = rows_of(r * 16, 16)
            total = sum_a[rows_of(xa * 32 + r * 16, 16), :] + got_b[rows, :].astype(F32)
            sum_b[rows, :] = total
            pass_b[rows, :] = total.astype(BF16)

        send(pass_b.at[rows_of((1 - xb) * 16, 16), :], got_c, as_sem.at[2], ar_sem.at[2], far_x)

    def outer_3():
        arrive(got_c, as_sem.at[2], ar_sem.at[2])
        pass_c[...] = (sum_b[rows_of(xb * 16, 16), :] + got_c[...].astype(F32)).astype(BF16)
        send(pass_c, got_d, as_sem.at[3], ar_sem.at[3], far_y)

    def outer_4():
        arrive(got_d, as_sem.at[3], ar_sem.at[3])
        rows = rows_of(row_c, 16)
        drift[rows, :] = (pass_c[...].astype(F32) + got_d[...].astype(F32)).astype(BF16)
        send(drift.at[rows, :], drift.at[rows, :], as_sem.at[4], ar_sem.at[4], far_x)

    def outer_5():
        arrive(drift.at[rows_of(row_b + (1 - xb) * 16, 16), :], as_sem.at[4], ar_sem.at[4])
        rows = rows_of(row_b, 32)
        send(drift.at[rows, :], drift.at[rows, :], as_sem.at[5], ar_sem.at[5], near_x)

    def outer_6():
        arrive(drift.at[rows_of(row_a + (1 - xa) * 32, 32), :], as_sem.at[5], ar_sem.at[5])
        rows = rows_of(row_a, 64)
        send(drift.at[rows, :], drift.at[rows, :], as_sem.at[6], ar_sem.at[6], sib)

    out_drift = pltpu.make_async_copy(drift, drift_hbm, out_sem.at[0])

    def outer_7():
        arrive(drift.at[rows_of((1 - core) * 64, 64), :], as_sem.at[6], ar_sem.at[6])
        out_drift.start()

    stat_recv[:, 8:128, :] = jnp.zeros((2, 120, TOK), F32)
    outer_0()

    def chunk_at(offset):
        return lax.rem(z + NZ + offset, NZ)

    def chunk_rows(offset):
        return pl.ds(aligned(chunk_at(offset), CHUNK), CHUNK)

    def project(chunk, tokens, first=False):
        rows = pl.ds(aligned(chunk, CHUNK), CHUNK)

        @pl.loop(0, 4)
        def _(n):
            cols = pl.ds(aligned(n, 256), 256)
            part = jnp.dot(ctx[tokens, rows], wbuf[rows, cols], preferred_element_type=F32)
            if first:
                proj[tokens, cols] = part
            else:
                proj[tokens, cols] += part

    def turn(tokens):
        @pl.loop(0, NZ)
        def _(n):
            cols = pl.ds(aligned(n, CHUNK), CHUNK)
            ctxt[cols, tokens] = ctx[tokens, cols].T

    own_tok, par_tok = pl.ds(0, TOK), pl.ds(TOK, TOK)
    loc_w.wait()
    loc_ctx.wait()
    project(z, own_tok, first=True)
    turn(own_tok)

    stages = (outer_1, outer_2)
    for hop in range(1, 4):
        froms = (chunk_at(-hop), chunk_at(hop))
        for u in range(4):
            for way in range(2):
                arrive(
                    wbuf.at[unit_rows(froms[way], u), :],
                    zs_sem.at[way, hop - 1, u],
                    zr_sem.at[way, hop - 1, u],
                )
                pass_on(hop, u, way, froms[way])
            if hop == 3 and u == 2:
                arrive(ctx.at[par_tok, :], ys_sem.at[2], yr_sem.at[2])
                project(z, par_tok, first=True)
                for near in (1, -1, 2, -2):
                    project(chunk_at(near), par_tok)
        for way in range(2):
            project(froms[way], own_tok)
            if hop == 3:
                project(froms[way], par_tok)
        if hop < 3:
            stages[hop - 1]()

    def project_part(owner, tokens):
        rows = pl.ds(pl.multiple_of(chunk_at(4) * CHUNK + owner * ROWS, ROWS), ROWS)

        @pl.loop(0, 4)
        def _(n):
            cols = pl.ds(aligned(n, 256), 256)
            proj[tokens, cols] += jnp.dot(
                ctx[tokens, rows], wbuf[rows, cols], preferred_element_type=F32
            )

    last = chunk_at(4)
    for u in range(4):
        arrive(wbuf.at[unit_rows(last, u), :], zs_sem.at[u % 2, 3, u], zr_sem.at[u % 2, 3, u])
        if u == 1:
            project_part(y, pl.ds(0, PAIR))
            loc_cot.wait()
            loc_gain.wait()
            arrive(cot.at[par_tok, :], ys_sem.at[3], yr_sem.at[3])

    gain = gain_buf[...]
    lane = lax.broadcasted_iota(jnp.int32, (UNIT, 128), 1)

    def stat_sem(half):
        return 4 if half == 1 else 11

    for half in (1, 0):
        project_part(other, pl.ds(half * TOK, TOK))

        @pl.loop(0, TOK // UNIT)
        def _(r):
            rows = rows_of(half * TOK + r * UNIT, UNIT)
            p = proj[rows, :]
            scaled = cot[rows, :].astype(F32) * gain
            square = jnp.sum(p * p, axis=1, keepdims=True)
            cross = jnp.sum(scaled * p, axis=1, keepdims=True)
            stat_own[rows, :] = jnp.where(lane == 0, square, jnp.where(lane == 1, cross, 0.0))

        stat_send[half] = stat_own[half * TOK : half * TOK + TOK, :].T[0:8, :]
        k = stat_sem(half)
        send(
            stat_send.at[half],
            stat_recv.at[1 - half, pl.ds(0, 8), :],
            ys_sem.at[k],
            yr_sem.at[k],
            pair,
        )

    outer_3()
    turn(par_tok)
    for half in range(2):
        k = stat_sem(1 - half)
        arrive(stat_recv.at[half, pl.ds(0, 8), :], ys_sem.at[k], yr_sem.at[k])
        stat_own[half * TOK : half * TOK + TOK, :] += stat_recv[half].T

        @pl.loop(0, TOK // UNIT)
        def _(r):
            rows = rows_of(half * TOK + r * UNIT, UNIT)
            stat = stat_own[rows, :] * (1.0 / D)
            inv = lax.rsqrt(stat[:, 0:1] + 1e-06)
            slope = inv * inv * stat[:, 1:2]
            scaled = cot[rows, :].astype(F32) * gain
            pg[rows, :] = (inv * (scaled - proj[rows, :] * slope)).astype(BF16)

    def grad_of(rows, dst):
        @pl.loop(0, 4)
        def _(n):
            cols = pl.ds(aligned(n, 256), 256)
            dst[:, cols] = jnp.dot(ctxt[rows, :], pg[:, cols], preferred_element_type=F32)

    def piece_rows(piece, size, offset=0):
        owner = other if piece == 0 else y
        return pl.ds(pl.multiple_of(owner * ROWS + offset, size), size)

    for piece in range(2):
        owner = other if piece == 0 else y
        rows = pl.ds(pl.multiple_of(chunk_at(4) * CHUNK + owner * ROWS, ROWS), ROWS)
        grad_of(rows, far.at[piece_rows(piece, ROWS), :])
        for way in range(2):
            half_send[way, piece] = far[
                piece_rows(piece, ROWS), way * 512 : way * 512 + 512
            ].astype(BF16)
            send(
                half_send.at[way, piece],
                half_recv.at[way, piece],
                hs_sem.at[way, piece],
                hr_sem.at[way, piece],
                ring[way],
            )

    def back(tokens, cols):
        return lax.dot_general(
            pg[tokens, :], wbuf[cols, :], (((1,), (1,)), ((), ())), preferred_element_type=F32
        )

    for q in range(4):
        @pl.loop(0, 2)
        def _(n):
            cols = pl.ds(pl.multiple_of(q * 512 + n * 256, 256), 256)
            cg_send[:, cols] = back(par_tok, cols).astype(BF16)

        cols = pl.ds(q * 512, 512)
        send(cg_send.at[:, cols], cg_recv.at[:, cols], ys_sem.at[5 + q], yr_sem.at[5 + q], pair)

    for way in range(2):
        grad_of(chunk_rows(3 if way == 0 else -3), parts.at[way, 0])

    def forward(hop, piece, t, way):
        n = 2 * piece + t
        rows = pl.ds(t * UNIT, UNIT)
        src = parts.at[way, 3 - hop]
        own = src[piece_rows(piece, UNIT, t * UNIT), :]
        if hop == 3:
            if t == 0:
                arrive(
                    half_recv.at[way, piece], hs_sem.at[way, piece], hr_sem.at[way, piece]
                )
            cut = slice(way * 512, way * 512 + 512)
            rest = slice(512 - way * 512, 1024 - way * 512)
            full_send[way, 0, n, :, cut] = (
                own[:, cut] + half_recv[way, piece, rows, :].astype(F32)
            ).astype(BF16)
            full_send[way, 0, n, :, rest] = own[:, rest].astype(BF16)
        else:
            arrive(
                full_recv.at[way, 2 - hop, n], fs_sem.at[way, 2 - hop, n], fr_sem.at[way, 2 - hop, n]
            )
            full_send[way, 3 - hop, n] = (
                own + full_recv[way, 2 - hop, n].astype(F32)
            ).astype(BF16)
        send(
            full_send.at[way, 3 - hop, n],
            full_recv.at[way, 3 - hop, n],
            fs_sem.at[way, 3 - hop, n],
            fr_sem.at[way, 3 - hop, n],
            ring[way],
        )

    def own_back():
        @pl.loop(0, NZ)
        def _(n):
            cols = pl.ds(aligned(n, 256), 256)
            cg_own[:, cols] = back(own_tok, cols)

    out_cg = pltpu.make_async_copy(cg_out, cg_hbm, out_sem.at[1])

    def finish_back():
        for q in range(4):
            cols = pl.ds(q * 512, 512)
            arrive(cg_recv.at[:, cols], ys_sem.at[5 + q], yr_sem.at[5 + q])

        @pl.loop(0, 16)
        def _(r):
            rows = rows_of(r * 16, 16)
            cg_out[rows, :] = (cg_own[rows, :] + cg_recv[rows, :].astype(F32)).astype(BF16)

        out_cg.start()

    def hop_of(hop, between):
        for piece in range(2):
            for t in range(2):
                for way in range(2):
                    forward(hop, piece, t, way)
            between[piece]()

    def next_parts(hop):
        for way in range(2):
            grad_of(chunk_rows(hop if way == 0 else -hop), parts.at[way, 3 - hop])

    def after_3a():
        next_parts(2)

    def after_3b():
        own_back()
        outer_4()

    def after_2a():
        next_parts(1)
        outer_5()

    def after_2b():
        grad_of(chunk_rows(0), far)
        outer_6()

    hop_of(3, (after_3a, after_3b))
    hop_of(2, (after_2a, after_2b))
    hop_of(1, (outer_7, finish_back))

    out_own = pltpu.make_async_copy(
        grad_out.at[0], grad_hbm.at[:, pl.ds(mine, HALF)], out_sem.at[2]
    )
    out_par = pltpu.make_async_copy(
        grad_out.at[1], grad_hbm.at[:, pl.ds(theirs, HALF)], out_sem.at[3]
    )
    for piece in range(2):
        for t in range(2):
            n = 2 * piece + t
            rows = pl.ds(t * UNIT, UNIT)
            total = far[piece_rows(piece, UNIT, t * UNIT), :]
            for way in range(2):
                arrive(full_recv.at[way, 2, n], fs_sem.at[way, 2, n], fr_sem.at[way, 2, n])
                total = total + full_recv[way, 2, n].astype(F32)
            if piece == 0:
                y_send[t] = total.astype(BF16)
                send(y_send.at[t], y_recv.at[t], ys_sem.at[9 + t], yr_sem.at[9 + t], pair)
            else:
                grad_out[0, rows, :] = total
    out_own.start()
    for t in range(2):
        arrive(y_recv.at[t], ys_sem.at[9 + t], yr_sem.at[9 + t])
        grad_out[1, t * UNIT : (t + 1) * UNIT, :] = y_recv[t].astype(F32)
    out_par.start()
    for copy in sends:
        copy.wait_send()
    for copy in (out_drift, out_cg, out_own, out_par):
        copy.wait()


def exchange(context, cotangent, gain, weight, frags, step):
    anywhere = pl.BlockSpec(memory_space=pl.ANY)
    in_hbm = pl.BlockSpec(memory_space=pltpu.HBM)
    dma = pltpu.SemaphoreType.DMA
    return pl.pallas_call(
        kernel,
        out_shape=(
            jax.ShapeDtypeStruct((TOK, D), BF16),
            jax.ShapeDtypeStruct((ROWS, D), F32),
            jax.ShapeDtypeStruct((ROWS, D), BF16),
        ),
        in_specs=[
            in_hbm,
            in_hbm,
            in_hbm,
            in_hbm,
            in_hbm,
            pl.BlockSpec(memory_space=pltpu.SMEM),
        ],
        out_specs=(anywhere, anywhere, anywhere),
        scratch_shapes=[
            pltpu.VMEM((D, HALF), BF16),
            pltpu.VMEM((PAIR, D), BF16),
            pltpu.VMEM((PAIR, HALF), BF16),
            pltpu.VMEM((1, HALF), F32),
            pltpu.VMEM((PAIR, HALF), F32),
            pltpu.VMEM((PAIR, HALF), BF16),
            pltpu.VMEM((D, PAIR), BF16),
            pltpu.VMEM((PAIR, 128), F32),
            pltpu.VMEM((2, 8, TOK), F32),
            pltpu.VMEM((2, 128, TOK), F32),
            pltpu.VMEM((CHUNK, HALF), F32),
            pltpu.VMEM((2, 3, CHUNK, HALF), F32),
            pltpu.VMEM((2, 2, ROWS, 512), BF16),
            pltpu.VMEM((2, 2, ROWS, 512), BF16),
            pltpu.VMEM((2, 3, 4, UNIT, HALF), BF16),
            pltpu.VMEM((2, 3, 4, UNIT, HALF), BF16),
            pltpu.VMEM((2, UNIT, HALF), BF16),
            pltpu.VMEM((2, UNIT, HALF), BF16),
            pltpu.VMEM((2, ROWS, HALF), F32),
            pltpu.VMEM((TOK, D), F32),
            pltpu.VMEM((TOK, D), BF16),
            pltpu.VMEM((TOK, D), BF16),
            pltpu.VMEM((TOK, D), BF16),
            pltpu.VMEM((NFRAG, ROWS, D), BF16),
            pltpu.VMEM((ROWS, D), BF16),
            pltpu.VMEM((64, D), F32),
            pltpu.VMEM((32, D), F32),
            pltpu.VMEM((64, D), BF16),
            pltpu.VMEM((32, D), BF16),
            pltpu.VMEM((16, D), BF16),
            pltpu.VMEM((64, D), BF16),
            pltpu.VMEM((32, D), BF16),
            pltpu.VMEM((16, D), BF16),
            pltpu.VMEM((16, D), BF16),
            pltpu.VMEM((ROWS, D), BF16),
            dma((5,)),
            dma((4,)),
            dma((2, 4, 4)),
            dma((2, 4, 4)),
            dma((12,)),
            dma((12,)),
            dma((2, 2)),
            dma((2, 2)),
            dma((2, 3, 4)),
            dma((2, 3, 4)),
            dma((7,)),
            dma((7,)),
        ],
        compiler_params=pltpu.CompilerParams(
            collective_id=0, has_side_effects=True, vmem_limit_bytes=46 * 2**20
        ),
        cost_estimate=pl.CostEstimate(
            flops=6 * TOK * D * D, bytes_accessed=8 * 2**20, transcendentals=PAIR
        ),
        name="exchange",
    )(*(pltpu.with_memory_space_constraint(a, pltpu.HBM) for a in (context, cotangent, gain, weight, frags)), step)


def finish_kernel(
    step_ref,
    cg_ref,
    grad_ref,
    drift_ref,
    one_ref,
    two_ref,
    weight_ref,
    anchors_ref,
    momenta_ref,
    cg_hbm,
    weight_hbm,
    one_hbm,
    two_hbm,
    anchor_hbm,
    momentum_hbm,
    weight_buf,
    one_buf,
    two_buf,
    anchor_buf,
    momentum_buf,
    sem,
):
    copies = []

    def put(src, dst):
        copy = pltpu.make_async_copy(src, dst, sem.at[len(copies)])
        copy.start()
        copies.append(copy)

    put(cg_ref, cg_hbm)
    step = step_ref[0]
    due = lax.rem(step, NFRAG)
    rate = rate_base + rate_base * jnp.minimum(step, 1000).astype(F32) / 1000.0
    for block in range(4):
        @pl.loop(0, 2)
        def _(r):
            rows = pl.ds(pl.multiple_of(block * 32 + r * 16, 16), 16)
            first = beta_one * one_ref[0, rows, :] + (1.0 - beta_one) * grad_ref[rows, :]
            grad = grad_ref[rows, :]
            second = beta_two * two_ref[0, rows, :] + (1.0 - beta_two) * grad * grad
            weight = weight_ref[0, rows, :].astype(F32)
            update = first / (jnp.sqrt(second) + adam_eps) + decay_rate * weight
            one_buf[rows, :] = first
            two_buf[rows, :] = second
            weight_buf[rows, :] = (weight - inner_rate * update).astype(BF16)

        rows = pl.ds(block * 32, 32)
        put(one_buf.at[rows, :], one_hbm.at[0, rows, :])
        put(two_buf.at[rows, :], two_hbm.at[0, rows, :])
        put(weight_buf.at[rows, :], weight_hbm.at[0, rows, :])

    for block in range(2):
        @pl.loop(0, 4)
        def _(r):
            rows = pl.ds(pl.multiple_of(block * 64 + r * 16, 16), 16)
            anchor = anchors_ref[due, rows, :].astype(F32)
            pseudo = anchor - drift_ref[rows, :].astype(F32) / N_ISLAND
            momentum = outer_mu * momenta_ref[due, rows, :] + pseudo
            momentum_buf[rows, :] = momentum
            anchor_buf[rows, :] = (anchor - rate * (pseudo + outer_mu * momentum)).astype(BF16)

        rows = pl.ds(block * 64, 64)
        put(momentum_buf.at[rows, :], momentum_hbm.at[rows, :])
        put(anchor_buf.at[rows, :], anchor_hbm.at[rows, :])
    for copy in copies:
        copy.wait()


def finish(step, *operands):
    inside = pl.BlockSpec(memory_space=pltpu.VMEM)
    anywhere = pl.BlockSpec(memory_space=pl.ANY)
    return pl.pallas_call(
        finish_kernel,
        out_shape=(
            jax.ShapeDtypeStruct((TOK, D), BF16),
            jax.ShapeDtypeStruct((1, ROWS, D), BF16),
            jax.ShapeDtypeStruct((1, ROWS, D), F32),
            jax.ShapeDtypeStruct((1, ROWS, D), F32),
            jax.ShapeDtypeStruct((ROWS, D), BF16),
            jax.ShapeDtypeStruct((ROWS, D), F32),
        ),
        in_specs=[pl.BlockSpec(memory_space=pltpu.SMEM)] + [inside] * 8,
        out_specs=(anywhere,) * 6,
        scratch_shapes=[
            pltpu.VMEM((ROWS, D), BF16),
            pltpu.VMEM((ROWS, D), F32),
            pltpu.VMEM((ROWS, D), F32),
            pltpu.VMEM((ROWS, D), BF16),
            pltpu.VMEM((ROWS, D), F32),
            pltpu.SemaphoreType.DMA((17,)),
        ],
        compiler_params=pltpu.CompilerParams(vmem_limit_bytes=16 * 2**20),
        cost_estimate=pl.CostEstimate(
            flops=30 * ROWS * D, bytes_accessed=12 * 2**20, transcendentals=ROWS * D
        ),
        name="finish",
    )(step, *operands)


def local(
    context,
    cotangent,
    norm_gain,
    out_weight,
    moment_one,
    moment_two,
    local_frags,
    anchors,
    outer_moment,
    outer_step,
):
    ctx_grad, weight_grad, drift = exchange(
        context, cotangent, norm_gain.reshape(1, D), out_weight, local_frags, outer_step
    )
    return finish(
        outer_step,
        ctx_grad,
        weight_grad,
        drift,
        moment_one,
        moment_two,
        out_weight,
        anchors,
        outer_moment,
    )


def solution(mesh):
    return jax.shard_map(
        local,
        mesh=mesh,
        in_specs=(
            P(("island", "fsdp"), None),
            P(("island", "fsdp"), None),
            P(),
            P("island", "fsdp", None),
            P("island", "fsdp", None),
            P("island", "fsdp", None),
            P("island", None, "fsdp", None),
            P(None, "fsdp", None),
            P(None, "fsdp", None),
            P(),
        ),
        out_specs=(
            P(("island", "fsdp"), None),
            P("island", "fsdp", None),
            P("island", "fsdp", None),
            P("island", "fsdp", None),
            P("fsdp", None),
            P("fsdp", None),
        ),
        check_vma=False,
    )
```

```python
import functools

import jax
import jax.numpy as jnp
from jax import lax
from jax.experimental import pallas as pl
from jax.experimental.pallas import tpu as pltpu
from jax.sharding import PartitionSpec as P

NFRAG = 2
N_ISLAND = 16

beta_one = 0.9
beta_two = 0.95
inner_rate = 0.01
decay_rate = 0.1
adam_eps = 1e-08
outer_mu = 0.9
rate_base = 0.35

NZ = 8
TOK = 256
PAIR = 512
D = 2048
HALF = 1024
ROWS = 128
CHUNK = 256
UNIT = 64

F32 = jnp.float32
BF16 = jnp.bfloat16
MESH = pl.DeviceIdType.MESH


def aligned(value, size):
    return pl.multiple_of(value * size, size)


def kernel(
    ctx_hbm,
    cot_hbm,
    gain_hbm,
    w_hbm,
    frag_hbm,
    step_ref,
    cg_hbm,
    grad_hbm,
    drift_hbm,
    wbuf,
    ctx,
    cot,
    gain_buf,
    proj,
    pg,
    ctxt,
    stat_own,
    stat_send,
    stat_recv,
    far,
    parts,
    half_send,
    half_recv,
    full_send,
    full_recv,
    y_send,
    y_recv,
    grad_out,
    cg_own,
    cg_send,
    cg_recv,
    cg_out,
    frag,
    sel,
    sum_a,
    sum_b,
    pass_a,
    pass_b,
    pass_c,
    got_a,
    got_b,
    got_c,
    got_d,
    drift,
    loc_sem,
    out_sem,
    zs_sem,
    zr_sem,
    ys_sem,
    yr_sem,
    hs_sem,
    hr_sem,
    fs_sem,
    fr_sem,
    as_sem,
    ar_sem,
):
    isl = lax.axis_index("island")
    fsd = lax.axis_index("fsdp")
    y = lax.rem(fsd, 2)
    z = lax.div(fsd, 2)
    core = lax.rem(isl, 2)
    x = lax.rem(lax.div(isl, 2), 4)
    yh = lax.div(isl, 8)
    xa = lax.rem(x, 2)
    xb = lax.div(x, 2)
    other = 1 - y
    up = (isl, lax.rem(z + 1, NZ) * 2 + y)
    down = (isl, lax.rem(z + NZ - 1, NZ) * 2 + y)
    ring = (up, down)
    pair = (isl, z * 2 + other)
    sib = (isl + 1 - 2 * core, fsd)
    near_x = (isl + 2 - 4 * xa, fsd)
    far_x = (isl + 6 - 4 * x, fsd)
    part = lax.rem(xa + xb, 2)
    far_y = (isl + 8 - 16 * yh, fsd)
    mine = aligned(y, HALF)
    theirs = aligned(other, HALF)

    sends = []

    def send(src, dst, ss, rs, dev):
        copy = pltpu.make_async_remote_copy(
            src_ref=src, dst_ref=dst, send_sem=ss, recv_sem=rs, device_id=dev, device_id_type=MESH
        )
        copy.start()
        sends.append(copy)

    def arrive(dst, ss, rs):
        pltpu.make_async_remote_copy(
            src_ref=dst, dst_ref=dst, send_sem=ss, recv_sem=rs, device_id=pair, device_id_type=MESH
        ).wait_recv()

    loc_w = pltpu.make_async_copy(
        w_hbm.at[0, :, pl.ds(mine, HALF)], wbuf.at[pl.ds(aligned(fsd, ROWS), ROWS), :], loc_sem.at[0]
    )
    loc_ctx = pltpu.make_async_copy(ctx_hbm, ctx.at[pl.ds(0, TOK), :], loc_sem.at[1])
    loc_cot = pltpu.make_async_copy(
        cot_hbm.at[:, pl.ds(mine, HALF)], cot.at[pl.ds(0, TOK), :], loc_sem.at[2]
    )
    loc_frag = pltpu.make_async_copy(frag_hbm.at[0], frag, loc_sem.at[3])
    loc_gain = pltpu.make_async_copy(gain_hbm.at[:, pl.ds(mine, HALF)], gain_buf, loc_sem.at[4])
    for copy in (loc_w, loc_frag, loc_ctx, loc_cot, loc_gain):
        copy.start()

    barrier = pltpu.get_barrier_semaphore()
    for dev in (up, down, pair, sib, near_x, far_x, far_y):
        pl.semaphore_signal(barrier, inc=1, device_id=dev, device_id_type=MESH)
    pl.semaphore_wait(barrier, 7)

    def unit_rows(z_from, u):
        owner = y if u < 2 else other
        return pl.ds(pl.multiple_of(z_from * CHUNK + owner * ROWS + (u % 2) * UNIT, UNIT), UNIT)

    for t in range(2):
        rows = pl.ds(t * UNIT, UNIT)
        send(
            w_hbm.at[0, rows, pl.ds(theirs, HALF)],
            wbuf.at[unit_rows(z, t), :],
            ys_sem.at[t],
            yr_sem.at[t],
            pair,
        )
        for way in range(2):
            send(
                w_hbm.at[0, rows, pl.ds(mine, HALF)],
                wbuf.at[unit_rows(z, t), :],
                zs_sem.at[way, 0, t],
                zr_sem.at[way, 0, t],
                ring[way],
            )

    def pass_on(hop, u, way, z_from):
        if hop < 3 or (u % 2) == way:
            ref = wbuf.at[unit_rows(z_from, u), :]
            send(ref, ref, zs_sem.at[way, hop, u], zr_sem.at[way, hop, u], ring[way])

    for t in range(2):
        arrive(wbuf.at[unit_rows(z, 2 + t), :], ys_sem.at[t], yr_sem.at[t])
        for way in range(2):
            pass_on(0, 2 + t, way, z)

    send(ctx_hbm, ctx.at[pl.ds(TOK, TOK), :], ys_sem.at[2], yr_sem.at[2], pair)
    send(
        cot_hbm.at[:, pl.ds(theirs, HALF)],
        cot.at[pl.ds(TOK, TOK), :],
        ys_sem.at[3],
        yr_sem.at[3],
        pair,
    )

    row_a = core * 64
    row_b = row_a + part * 32
    row_c = row_b + xb * 16

    def rows_of(start, size):
        return pl.ds(pl.multiple_of(start, size), size)

    def outer_0():
        loc_frag.wait()
        due = jnp.full((16, D), jnp.bitwise_and(step_ref[0], 1), jnp.int32)

        @pl.loop(0, 8)
        def _(r):
            rows = rows_of(r * 16, 16)
            sel[rows, :] = jnp.where(
                due == 0, frag[0, rows, :].astype(F32), frag[1, rows, :].astype(F32)
            ).astype(BF16)

        send(sel.at[rows_of((1 - core) * 64, 64), :], got_a, as_sem.at[0], ar_sem.at[0], sib)

    def outer_1():
        arrive(got_a, as_sem.at[0], ar_sem.at[0])

        @pl.loop(0, 4)
        def _(r):
            rows = rows_of(r * 16, 16)
            total = sel[rows_of(row_a + r * 16, 16), :].astype(F32) + got_a[rows, :].astype(F32)
            sum_a[rows, :] = total
            pass_a[rows, :] = total.astype(BF16)

        send(pass_a.at[rows_of((1 - part) * 32, 32), :], got_b, as_sem.at[1], ar_sem.at[1], near_x)

    def outer_2():
        arrive(got_b, as_sem.at[1], ar_sem.at[1])

        @pl.loop(0, 2)
        def _(r):
            rows = rows_of(r * 16, 16)
            total = sum_a[rows_of(part * 32 + r * 16, 16), :] + got_b[rows, :].astype(F32)
            sum_b[rows, :] = total
            pass_b[rows, :] = total.astype(BF16)

        send(pass_b.at[rows_of((1 - xb) * 16, 16), :], got_c, as_sem.at[2], ar_sem.at[2], far_x)

    def outer_3():
        arrive(got_c, as_sem.at[2], ar_sem.at[2])
        pass_c[...] = (sum_b[rows_of(xb * 16, 16), :] + got_c[...].astype(F32)).astype(BF16)
        send(pass_c, got_d, as_sem.at[3], ar_sem.at[3], far_y)

    def outer_4():
        arrive(got_d, as_sem.at[3], ar_sem.at[3])
        rows = rows_of(row_c, 16)
        drift[rows, :] = (pass_c[...].astype(F32) + got_d[...].astype(F32)).astype(BF16)
        send(drift.at[rows, :], drift.at[rows, :], as_sem.at[4], ar_sem.at[4], far_x)

    def outer_5():
        arrive(drift.at[rows_of(row_b + (1 - xb) * 16, 16), :], as_sem.at[4], ar_sem.at[4])
        rows = rows_of(row_b, 32)
        send(drift.at[rows, :], drift.at[rows, :], as_sem.at[5], ar_sem.at[5], near_x)

    def outer_6():
        arrive(drift.at[rows_of(row_a + (1 - part) * 32, 32), :], as_sem.at[5], ar_sem.at[5])
        rows = rows_of(row_a, 64)
        send(drift.at[rows, :], drift.at[rows, :], as_sem.at[6], ar_sem.at[6], sib)

    out_drift = pltpu.make_async_copy(drift, drift_hbm, out_sem.at[0])

    def outer_7():
        arrive(drift.at[rows_of((1 - core) * 64, 64), :], as_sem.at[6], ar_sem.at[6])
        out_drift.start()

    stat_recv[:, 8:128, :] = jnp.zeros((2, 120, TOK), F32)
    stat_send[...] = jnp.zeros((2, 8, TOK), F32)
    outer_0()

    def chunk_at(offset):
        return lax.rem(z + NZ + offset, NZ)

    def chunk_rows(offset):
        return pl.ds(aligned(chunk_at(offset), CHUNK), CHUNK)

    def project(chunk, tokens, first=False):
        rows = pl.ds(aligned(chunk, CHUNK), CHUNK)

        @pl.loop(0, 4, unroll=True)
        def _(n):
            cols = pl.ds(aligned(n, 256), 256)
            part = jnp.dot(ctx[tokens, rows], wbuf[rows, cols], preferred_element_type=F32)
            if first:
                proj[tokens, cols] = part
            else:
                proj[tokens, cols] += part

    def turn(tokens):
        @pl.loop(0, NZ)
        def _(n):
            cols = pl.ds(aligned(n, CHUNK), CHUNK)
            ctxt[cols, tokens] = ctx[tokens, cols].T

    own_tok, par_tok = pl.ds(0, TOK), pl.ds(TOK, TOK)
    loc_w.wait()
    loc_ctx.wait()
    project(z, own_tok, first=True)
    turn(own_tok)

    stages = (outer_1, outer_2)
    for hop in range(1, 4):
        froms = (chunk_at(-hop), chunk_at(hop))
        for u in range(4):
            for way in range(2):
                arrive(
                    wbuf.at[unit_rows(froms[way], u), :],
                    zs_sem.at[way, hop - 1, u],
                    zr_sem.at[way, hop - 1, u],
                )
                pass_on(hop, u, way, froms[way])
            if hop == 3 and u == 2:
                arrive(ctx.at[par_tok, :], ys_sem.at[2], yr_sem.at[2])
                project(z, par_tok, first=True)
                for near in (1, -1, 2, -2):
                    project(chunk_at(near), par_tok)
        for way in range(2):
            project(froms[way], own_tok)
            if hop == 3:
                project(froms[way], par_tok)
        if hop < 3:
            stages[hop - 1]()

    def project_part(owner, tokens):
        rows = pl.ds(pl.multiple_of(chunk_at(4) * CHUNK + owner * ROWS, ROWS), ROWS)

        @pl.loop(0, 4, unroll=True)
        def _(n):
            cols = pl.ds(aligned(n, 256), 256)
            proj[tokens, cols] += jnp.dot(
                ctx[tokens, rows], wbuf[rows, cols], preferred_element_type=F32
            )

    last = chunk_at(4)
    for u in range(4):
        arrive(wbuf.at[unit_rows(last, u), :], zs_sem.at[u % 2, 3, u], zr_sem.at[u % 2, 3, u])
        if u == 1:
            project_part(y, pl.ds(0, PAIR))
            loc_cot.wait()
            loc_gain.wait()
            arrive(cot.at[par_tok, :], ys_sem.at[3], yr_sem.at[3])

    gain = gain_buf[...]

    def stat_sem(half):
        return 4 if half == 1 else 11

    for half in (1, 0):
        project_part(other, pl.ds(half * TOK, TOK))

        @pl.loop(0, TOK // UNIT, unroll=True)
        def _(r):
            rows = rows_of(half * TOK + r * UNIT, UNIT)
            p = proj[rows, :]
            scaled = cot[rows, :].astype(F32) * gain
            square, cross = p * p, scaled * p
            lanes = [slice(128 * i, 128 * i + 128) for i in range(HALF // 128)]
            stat_own[0, rows, :] = sum(square[:, i] for i in lanes)
            stat_own[1, rows, :] = sum(cross[:, i] for i in lanes)

        for n in range(2):
            turned = stat_own[n, half * TOK : half * TOK + TOK, :].T
            stat_send[half, n : n + 1, :] = jnp.sum(turned, axis=0, keepdims=True)
        k = stat_sem(half)
        send(
            stat_send.at[half],
            stat_recv.at[1 - half, pl.ds(0, 8), :],
            ys_sem.at[k],
            yr_sem.at[k],
            pair,
        )

    outer_3()
    turn(par_tok)
    for half in range(2):
        k = stat_sem(1 - half)
        arrive(stat_recv.at[half, pl.ds(0, 8), :], ys_sem.at[k], yr_sem.at[k])
        stat_recv[half, 0:2, :] += stat_send[half, 0:2, :]
        stat_own[0, half * TOK : half * TOK + TOK, :] = stat_recv[half].T

        @pl.loop(0, TOK // UNIT, unroll=True)
        def _(r):
            rows = rows_of(half * TOK + r * UNIT, UNIT)
            stat = stat_own[0, rows, :] * (1.0 / D)
            inv = lax.rsqrt(stat[:, 0:1] + 1e-06)
            slope = inv * inv * stat[:, 1:2]
            scaled = cot[rows, :].astype(F32) * gain
            pg[rows, :] = (inv * (scaled - proj[rows, :] * slope)).astype(BF16)

    def grad_of(rows, dst):
        @pl.loop(0, 4, unroll=True)
        def _(n):
            cols = pl.ds(aligned(n, 256), 256)
            dst[:, cols] = jnp.dot(ctxt[rows, :], pg[:, cols], preferred_element_type=F32)

    def piece_rows(piece, size, offset=0):
        owner = other if piece == 0 else y
        return pl.ds(pl.multiple_of(owner * ROWS + offset, size), size)

    for piece in range(2):
        owner = other if piece == 0 else y
        rows = pl.ds(pl.multiple_of(chunk_at(4) * CHUNK + owner * ROWS, ROWS), ROWS)
        grad_of(rows, far.at[piece_rows(piece, ROWS), :])
        for way in range(2):
            half_send[way, piece] = far[
                piece_rows(piece, ROWS), way * 512 : way * 512 + 512
            ].astype(BF16)
            send(
                half_send.at[way, piece],
                half_recv.at[way, piece],
                hs_sem.at[way, piece],
                hr_sem.at[way, piece],
                ring[way],
            )

    def back(tokens, cols):
        return lax.dot_general(
            pg[tokens, :], wbuf[cols, :], (((1,), (1,)), ((), ())), preferred_element_type=F32
        )

    for q in range(4):
        @pl.loop(0, 2)
        def _(n):
            cols = pl.ds(pl.multiple_of(q * 512 + n * 256, 256), 256)
            cg_send[:, cols] = back(par_tok, cols).astype(BF16)

        cols = pl.ds(q * 512, 512)
        send(cg_send.at[:, cols], cg_recv.at[:, cols], ys_sem.at[5 + q], yr_sem.at[5 + q], pair)

    for way in range(2):
        grad_of(chunk_rows(3 if way == 0 else -3), parts.at[way, 0])

    def forward(hop, piece, t, way):
        n = 2 * piece + t
        rows = pl.ds(t * UNIT, UNIT)
        src = parts.at[way, 3 - hop]
        own = src[piece_rows(piece, UNIT, t * UNIT), :]
        if hop == 3:
            if t == 0:
                arrive(
                    half_recv.at[way, piece], hs_sem.at[way, piece], hr_sem.at[way, piece]
                )
            cut = slice(way * 512, way * 512 + 512)
            rest = slice(512 - way * 512, 1024 - way * 512)
            full_send[way, 0, n, :, cut] = (
                own[:, cut] + half_recv[way, piece, rows, :].astype(F32)
            ).astype(BF16)
            full_send[way, 0, n, :, rest] = own[:, rest].astype(BF16)
        else:
            arrive(
                full_recv.at[way, 2 - hop, n], fs_sem.at[way, 2 - hop, n], fr_sem.at[way, 2 - hop, n]
            )
            full_send[way, 3 - hop, n] = (
                own + full_recv[way, 2 - hop, n].astype(F32)
            ).astype(BF16)
        send(
            full_send.at[way, 3 - hop, n],
            full_recv.at[way, 3 - hop, n],
            fs_sem.at[way, 3 - hop, n],
            fr_sem.at[way, 3 - hop, n],
            ring[way],
        )

    def own_back():
        @pl.loop(0, NZ)
        def _(n):
            cols = pl.ds(aligned(n, 256), 256)
            cg_own[:, cols] = back(own_tok, cols)

    out_cg = pltpu.make_async_copy(cg_out, cg_hbm, out_sem.at[1])

    def finish_back():
        for q in range(4):
            cols = pl.ds(q * 512, 512)
            arrive(cg_recv.at[:, cols], ys_sem.at[5 + q], yr_sem.at[5 + q])

        @pl.loop(0, 16)
        def _(r):
            rows = rows_of(r * 16, 16)
            cg_out[rows, :] = (cg_own[rows, :] + cg_recv[rows, :].astype(F32)).astype(BF16)

        out_cg.start()

    def hop_of(hop, between):
        for piece in range(2):
            for t in range(2):
                for way in range(2):
                    forward(hop, piece, t, way)
            between[piece]()

    def next_parts(hop):
        for way in range(2):
            grad_of(chunk_rows(hop if way == 0 else -hop), parts.at[way, 3 - hop])

    def after_3a():
        next_parts(2)

    def after_3b():
        own_back()
        outer_4()

    def after_2a():
        next_parts(1)
        outer_5()

    def after_2b():
        grad_of(chunk_rows(0), far)
        outer_6()

    hop_of(3, (after_3a, after_3b))
    hop_of(2, (after_2a, after_2b))
    hop_of(1, (outer_7, finish_back))

    out_own = pltpu.make_async_copy(
        grad_out.at[0], grad_hbm.at[:, pl.ds(mine, HALF)], out_sem.at[2]
    )
    out_par = pltpu.make_async_copy(
        grad_out.at[1], grad_hbm.at[:, pl.ds(theirs, HALF)], out_sem.at[3]
    )
    for piece in range(2):
        for t in range(2):
            n = 2 * piece + t
            rows = pl.ds(t * UNIT, UNIT)
            total = far[piece_rows(piece, UNIT, t * UNIT), :]
            for way in range(2):
                arrive(full_recv.at[way, 2, n], fs_sem.at[way, 2, n], fr_sem.at[way, 2, n])
                total = total + full_recv[way, 2, n].astype(F32)
            if piece == 0:
                y_send[t] = total.astype(BF16)
                send(y_send.at[t], y_recv.at[t], ys_sem.at[9 + t], yr_sem.at[9 + t], pair)
            else:
                grad_out[0, rows, :] = total
    out_own.start()
    for t in range(2):
        arrive(y_recv.at[t], ys_sem.at[9 + t], yr_sem.at[9 + t])
        grad_out[1, t * UNIT : (t + 1) * UNIT, :] = y_recv[t].astype(F32)
    out_par.start()
    for copy in sends:
        copy.wait_send()
    for copy in (out_drift, out_cg, out_own, out_par):
        copy.wait()


def exchange(context, cotangent, gain, weight, frags, step):
    anywhere = pl.BlockSpec(memory_space=pl.ANY)
    in_hbm = pl.BlockSpec(memory_space=pltpu.HBM)
    dma = pltpu.SemaphoreType.DMA
    return pl.pallas_call(
        kernel,
        out_shape=(
            jax.ShapeDtypeStruct((TOK, D), BF16),
            jax.ShapeDtypeStruct((ROWS, D), F32),
            jax.ShapeDtypeStruct((ROWS, D), BF16),
        ),
        in_specs=[
            in_hbm,
            in_hbm,
            in_hbm,
            in_hbm,
            in_hbm,
            pl.BlockSpec(memory_space=pltpu.SMEM),
        ],
        out_specs=(anywhere, anywhere, anywhere),
        scratch_shapes=[
            pltpu.VMEM((D, HALF), BF16),
            pltpu.VMEM((PAIR, D), BF16),
            pltpu.VMEM((PAIR, HALF), BF16),
            pltpu.VMEM((1, HALF), F32),
            pltpu.VMEM((PAIR, HALF), F32),
            pltpu.VMEM((PAIR, HALF), BF16),
            pltpu.VMEM((D, PAIR), BF16),
            pltpu.VMEM((2, PAIR, 128), F32),
            pltpu.VMEM((2, 8, TOK), F32),
            pltpu.VMEM((2, 128, TOK), F32),
            pltpu.VMEM((CHUNK, HALF), F32),
            pltpu.VMEM((2, 3, CHUNK, HALF), F32),
            pltpu.VMEM((2, 2, ROWS, 512), BF16),
            pltpu.VMEM((2, 2, ROWS, 512), BF16),
            pltpu.VMEM((2, 3, 4, UNIT, HALF), BF16),
            pltpu.VMEM((2, 3, 4, UNIT, HALF), BF16),
            pltpu.VMEM((2, UNIT, HALF), BF16),
            pltpu.VMEM((2, UNIT, HALF), BF16),
            pltpu.VMEM((2, ROWS, HALF), F32),
            pltpu.VMEM((TOK, D), F32),
            pltpu.VMEM((TOK, D), BF16),
            pltpu.VMEM((TOK, D), BF16),
            pltpu.VMEM((TOK, D), BF16),
            pltpu.VMEM((NFRAG, ROWS, D), BF16),
            pltpu.VMEM((ROWS, D), BF16),
            pltpu.VMEM((64, D), F32),
            pltpu.VMEM((32, D), F32),
            pltpu.VMEM((64, D), BF16),
            pltpu.VMEM((32, D), BF16),
            pltpu.VMEM((16, D), BF16),
            pltpu.VMEM((64, D), BF16),
            pltpu.VMEM((32, D), BF16),
            pltpu.VMEM((16, D), BF16),
            pltpu.VMEM((16, D), BF16),
            pltpu.VMEM((ROWS, D), BF16),
            dma((5,)),
            dma((4,)),
            dma((2, 4, 4)),
            dma((2, 4, 4)),
            dma((12,)),
            dma((12,)),
            dma((2, 2)),
            dma((2, 2)),
            dma((2, 3, 4)),
            dma((2, 3, 4)),
            dma((7,)),
            dma((7,)),
        ],
        compiler_params=pltpu.CompilerParams(
            collective_id=0, has_side_effects=True, vmem_limit_bytes=46 * 2**20
        ),
        cost_estimate=pl.CostEstimate(
            flops=6 * TOK * D * D, bytes_accessed=8 * 2**20, transcendentals=PAIR
        ),
        name="exchange",
    )(*(pltpu.with_memory_space_constraint(a, pltpu.HBM) for a in (context, cotangent, gain, weight, frags)), step)


def finish_kernel(
    step_ref,
    cg_ref,
    grad_ref,
    drift_ref,
    one_ref,
    two_ref,
    weight_ref,
    anchors_ref,
    momenta_ref,
    cg_hbm,
    weight_hbm,
    one_hbm,
    two_hbm,
    anchor_hbm,
    momentum_hbm,
    weight_buf,
    one_buf,
    two_buf,
    anchor_buf,
    momentum_buf,
    sem,
):
    copies = []

    def put(src, dst):
        copy = pltpu.make_async_copy(src, dst, sem.at[len(copies)])
        copy.start()
        copies.append(copy)

    put(cg_ref, cg_hbm)
    step = step_ref[0]
    due = lax.rem(step, NFRAG)
    rate = rate_base + rate_base * jnp.minimum(step, 1000).astype(F32) / 1000.0
    for block in range(2):
        @pl.loop(0, 4)
        def _(r):
            rows = pl.ds(pl.multiple_of(block * 64 + r * 16, 16), 16)
            anchor = anchors_ref[due, rows, :].astype(F32)
            pseudo = anchor - drift_ref[rows, :].astype(F32) / N_ISLAND
            momentum = outer_mu * momenta_ref[due, rows, :] + pseudo
            momentum_buf[rows, :] = momentum
            anchor_buf[rows, :] = (anchor - rate * (pseudo + outer_mu * momentum)).astype(BF16)

        rows = pl.ds(block * 64, 64)
        put(momentum_buf.at[rows, :], momentum_hbm.at[rows, :])
        put(anchor_buf.at[rows, :], anchor_hbm.at[rows, :])
    for block in range(4):
        @pl.loop(0, 2, unroll=True)
        def _(r):
            rows = pl.ds(pl.multiple_of(block * 32 + r * 16, 16), 16)
            first = beta_one * one_ref[0, rows, :] + (1.0 - beta_one) * grad_ref[rows, :]
            grad = grad_ref[rows, :]
            second = beta_two * two_ref[0, rows, :] + (1.0 - beta_two) * grad * grad
            weight = weight_ref[0, rows, :].astype(F32)
            update = first / (jnp.sqrt(second) + adam_eps) + decay_rate * weight
            one_buf[rows, :] = first
            two_buf[rows, :] = second
            weight_buf[rows, :] = (weight - inner_rate * update).astype(BF16)

        rows = pl.ds(block * 32, 32)
        put(one_buf.at[rows, :], one_hbm.at[0, rows, :])
        put(two_buf.at[rows, :], two_hbm.at[0, rows, :])
        put(weight_buf.at[rows, :], weight_hbm.at[0, rows, :])

    for copy in copies:
        copy.wait()


def finish(step, *operands):
    inside = pl.BlockSpec(memory_space=pltpu.VMEM)
    anywhere = pl.BlockSpec(memory_space=pl.ANY)
    return pl.pallas_call(
        finish_kernel,
        out_shape=(
            jax.ShapeDtypeStruct((TOK, D), BF16),
            jax.ShapeDtypeStruct((1, ROWS, D), BF16),
            jax.ShapeDtypeStruct((1, ROWS, D), F32),
            jax.ShapeDtypeStruct((1, ROWS, D), F32),
            jax.ShapeDtypeStruct((ROWS, D), BF16),
            jax.ShapeDtypeStruct((ROWS, D), F32),
        ),
        in_specs=[pl.BlockSpec(memory_space=pltpu.SMEM)] + [inside] * 8,
        out_specs=(anywhere,) * 6,
        scratch_shapes=[
            pltpu.VMEM((ROWS, D), BF16),
            pltpu.VMEM((ROWS, D), F32),
            pltpu.VMEM((ROWS, D), F32),
            pltpu.VMEM((ROWS, D), BF16),
            pltpu.VMEM((ROWS, D), F32),
            pltpu.SemaphoreType.DMA((17,)),
        ],
        compiler_params=pltpu.CompilerParams(vmem_limit_bytes=16 * 2**20),
        cost_estimate=pl.CostEstimate(
            flops=30 * ROWS * D, bytes_accessed=12 * 2**20, transcendentals=ROWS * D
        ),
        name="finish",
    )(step, *operands)


def local(
    context,
    cotangent,
    norm_gain,
    out_weight,
    moment_one,
    moment_two,
    local_frags,
    anchors,
    outer_moment,
    outer_step,
):
    ctx_grad, weight_grad, drift = exchange(
        context, cotangent, norm_gain.reshape(1, D), out_weight, local_frags, outer_step
    )
    return finish(
        outer_step,
        ctx_grad,
        weight_grad,
        drift,
        moment_one,
        moment_two,
        out_weight,
        anchors,
        outer_moment,
    )


def solution(mesh):
    return jax.shard_map(
        local,
        mesh=mesh,
        in_specs=(
            P(("island", "fsdp"), None),
            P(("island", "fsdp"), None),
            P(),
            P("island", "fsdp", None),
            P("island", "fsdp", None),
            P("island", "fsdp", None),
            P("island", None, "fsdp", None),
            P(None, "fsdp", None),
            P(None, "fsdp", None),
            P(),
        ),
        out_specs=(
            P(("island", "fsdp"), None),
            P("island", "fsdp", None),
            P("island", "fsdp", None),
            P("island", "fsdp", None),
            P("fsdp", None),
            P("fsdp", None),
        ),
        check_vma=False,
    )
```

```python
import functools

import jax
import jax.numpy as jnp
from jax import lax
from jax.experimental import pallas as pl
from jax.experimental.pallas import tpu as pltpu
from jax.sharding import PartitionSpec as P

NFRAG = 2
N_ISLAND = 16

beta_one = 0.9
beta_two = 0.95
inner_rate = 0.01
decay_rate = 0.1
adam_eps = 1e-08
outer_mu = 0.9
rate_base = 0.35

NZ = 8
TOK = 256
PAIR = 512
D = 2048
HALF = 1024
ROWS = 128
CHUNK = 256
UNIT = 64

F32 = jnp.float32
BF16 = jnp.bfloat16
MESH = pl.DeviceIdType.MESH


def aligned(value, size):
    return pl.multiple_of(value * size, size)


def kernel(
    ctx_hbm,
    cot_hbm,
    gain_hbm,
    w_hbm,
    frag_hbm,
    step_ref,
    cg_ref,
    grad_ref,
    drift_hbm,
    wbuf,
    ctx,
    cot,
    gain_buf,
    proj,
    pg,
    ctxt,
    stat_own,
    stat_send,
    stat_recv,
    far,
    parts,
    half_send,
    half_recv,
    full_send,
    full_recv,
    y_send,
    y_recv,
    cg_own,
    cg_send,
    cg_recv,
    frag,
    sel,
    sum_a,
    sum_b,
    pass_a,
    pass_b,
    pass_c,
    got_a,
    got_b,
    got_c,
    got_d,
    drift,
    loc_sem,
    out_sem,
    zs_sem,
    zr_sem,
    ys_sem,
    yr_sem,
    hs_sem,
    hr_sem,
    fs_sem,
    fr_sem,
    as_sem,
    ar_sem,
):
    isl = lax.axis_index("island")
    fsd = lax.axis_index("fsdp")
    y = lax.rem(fsd, 2)
    z = lax.div(fsd, 2)
    core = lax.rem(isl, 2)
    x = lax.rem(lax.div(isl, 2), 4)
    yh = lax.div(isl, 8)
    xa = lax.rem(x, 2)
    xb = lax.div(x, 2)
    other = 1 - y
    up = (isl, lax.rem(z + 1, NZ) * 2 + y)
    down = (isl, lax.rem(z + NZ - 1, NZ) * 2 + y)
    ring = (up, down)
    pair = (isl, z * 2 + other)
    sib = (isl + 1 - 2 * core, fsd)
    near_x = (isl + 2 - 4 * xa, fsd)
    far_x = (isl + 6 - 4 * x, fsd)
    part = lax.rem(xa + xb, 2)
    far_y = (isl + 8 - 16 * yh, fsd)
    mine = aligned(y, HALF)
    theirs = aligned(other, HALF)

    sends = []

    def send(src, dst, ss, rs, dev):
        copy = pltpu.make_async_remote_copy(
            src_ref=src, dst_ref=dst, send_sem=ss, recv_sem=rs, device_id=dev, device_id_type=MESH
        )
        copy.start()
        sends.append(copy)

    def arrive(dst, ss, rs):
        pltpu.make_async_remote_copy(
            src_ref=dst, dst_ref=dst, send_sem=ss, recv_sem=rs, device_id=pair, device_id_type=MESH
        ).wait_recv()

    barrier = pltpu.get_barrier_semaphore()
    for dev in (far_x, up, down, far_y, pair, near_x, sib):
        pl.semaphore_signal(barrier, inc=1, device_id=dev, device_id_type=MESH)

    loc_w = pltpu.make_async_copy(
        w_hbm.at[0, :, pl.ds(mine, HALF)], wbuf.at[pl.ds(aligned(fsd, ROWS), ROWS), :], loc_sem.at[0]
    )
    loc_ctx = pltpu.make_async_copy(ctx_hbm, ctx.at[pl.ds(0, TOK), :], loc_sem.at[1])
    loc_cot = pltpu.make_async_copy(
        cot_hbm.at[:, pl.ds(mine, HALF)], cot.at[pl.ds(0, TOK), :], loc_sem.at[2]
    )
    loc_frag = pltpu.make_async_copy(frag_hbm.at[0], frag, loc_sem.at[3])
    loc_gain = pltpu.make_async_copy(gain_hbm.at[:, pl.ds(mine, HALF)], gain_buf, loc_sem.at[4])
    for copy in (loc_w, loc_frag, loc_ctx, loc_cot, loc_gain):
        copy.start()

    pl.semaphore_wait(barrier, 7)

    def unit_rows(z_from, u):
        owner = y if u < 2 else other
        return pl.ds(pl.multiple_of(z_from * CHUNK + owner * ROWS + (u % 2) * UNIT, UNIT), UNIT)

    for t in range(2):
        rows = pl.ds(t * UNIT, UNIT)
        send(
            w_hbm.at[0, rows, pl.ds(theirs, HALF)],
            wbuf.at[unit_rows(z, t), :],
            ys_sem.at[t],
            yr_sem.at[t],
            pair,
        )
        for way in range(2):
            send(
                w_hbm.at[0, rows, pl.ds(mine, HALF)],
                wbuf.at[unit_rows(z, t), :],
                zs_sem.at[way, 0, t],
                zr_sem.at[way, 0, t],
                ring[way],
            )

    def pass_on(hop, u, way, z_from):
        if hop < 3 or (u % 2) == way:
            ref = wbuf.at[unit_rows(z_from, u), :]
            send(ref, ref, zs_sem.at[way, hop, u], zr_sem.at[way, hop, u], ring[way])

    for t in range(2):
        arrive(wbuf.at[unit_rows(z, 2 + t), :], ys_sem.at[t], yr_sem.at[t])
        for way in range(2):
            pass_on(0, 2 + t, way, z)

    send(ctx_hbm, ctx.at[pl.ds(TOK, TOK), :], ys_sem.at[2], yr_sem.at[2], pair)
    send(
        cot_hbm.at[:, pl.ds(theirs, HALF)],
        cot.at[pl.ds(TOK, TOK), :],
        ys_sem.at[3],
        yr_sem.at[3],
        pair,
    )

    row_a = core * 64
    row_b = row_a + part * 32
    row_c = row_b + xb * 16

    def rows_of(start, size):
        return pl.ds(pl.multiple_of(start, size), size)

    def outer_0():
        loc_frag.wait()
        due = jnp.full((16, D), jnp.bitwise_and(step_ref[0], 1), jnp.int32)

        @pl.loop(0, 8)
        def _(r):
            rows = rows_of(r * 16, 16)
            sel[rows, :] = jnp.where(
                due == 0, frag[0, rows, :].astype(F32), frag[1, rows, :].astype(F32)
            ).astype(BF16)

        send(sel.at[rows_of((1 - core) * 64, 64), :], got_a, as_sem.at[0], ar_sem.at[0], sib)

    def outer_1():
        arrive(got_a, as_sem.at[0], ar_sem.at[0])

        @pl.loop(0, 4)
        def _(r):
            rows = rows_of(r * 16, 16)
            total = sel[rows_of(row_a + r * 16, 16), :].astype(F32) + got_a[rows, :].astype(F32)
            sum_a[rows, :] = total
            pass_a[rows, :] = total.astype(BF16)

        send(pass_a.at[rows_of((1 - part) * 32, 32), :], got_b, as_sem.at[1], ar_sem.at[1], near_x)

    def outer_2():
        arrive(got_b, as_sem.at[1], ar_sem.at[1])

        @pl.loop(0, 2)
        def _(r):
            rows = rows_of(r * 16, 16)
            total = sum_a[rows_of(part * 32 + r * 16, 16), :] + got_b[rows, :].astype(F32)
            sum_b[rows, :] = total
            pass_b[rows, :] = total.astype(BF16)

        send(pass_b.at[rows_of((1 - xb) * 16, 16), :], got_c, as_sem.at[2], ar_sem.at[2], far_x)

    def outer_3():
        arrive(got_c, as_sem.at[2], ar_sem.at[2])
        pass_c[...] = (sum_b[rows_of(xb * 16, 16), :] + got_c[...].astype(F32)).astype(BF16)
        send(pass_c, got_d, as_sem.at[3], ar_sem.at[3], far_y)

    def outer_4():
        arrive(got_d, as_sem.at[3], ar_sem.at[3])
        rows = rows_of(row_c, 16)
        drift[rows, :] = (pass_c[...].astype(F32) + got_d[...].astype(F32)).astype(BF16)
        send(drift.at[rows, :], drift.at[rows, :], as_sem.at[4], ar_sem.at[4], far_x)

    def outer_5():
        arrive(drift.at[rows_of(row_b + (1 - xb) * 16, 16), :], as_sem.at[4], ar_sem.at[4])
        rows = rows_of(row_b, 32)
        send(drift.at[rows, :], drift.at[rows, :], as_sem.at[5], ar_sem.at[5], near_x)

    def outer_6():
        arrive(drift.at[rows_of(row_a + (1 - part) * 32, 32), :], as_sem.at[5], ar_sem.at[5])
        rows = rows_of(row_a, 64)
        send(drift.at[rows, :], drift.at[rows, :], as_sem.at[6], ar_sem.at[6], sib)

    out_drift = pltpu.make_async_copy(drift, drift_hbm, out_sem.at[0])

    def outer_7():
        arrive(drift.at[rows_of((1 - core) * 64, 64), :], as_sem.at[6], ar_sem.at[6])
        out_drift.start()

    stat_recv[:, 8:128, :] = jnp.zeros((2, 120, TOK), F32)
    stat_send[...] = jnp.zeros((2, 8, TOK), F32)
    outer_0()

    def chunk_at(offset):
        return lax.rem(z + NZ + offset, NZ)

    def chunk_rows(offset):
        return pl.ds(aligned(chunk_at(offset), CHUNK), CHUNK)

    def project(chunk, tokens, first=False):
        rows = pl.ds(aligned(chunk, CHUNK), CHUNK)

        @pl.loop(0, 4, unroll=True)
        def _(n):
            cols = pl.ds(aligned(n, 256), 256)
            part = jnp.dot(ctx[tokens, rows], wbuf[rows, cols], preferred_element_type=F32)
            if first:
                proj[tokens, cols] = part
            else:
                proj[tokens, cols] += part

    def turn(tokens):
        @pl.loop(0, NZ)
        def _(n):
            cols = pl.ds(aligned(n, CHUNK), CHUNK)
            ctxt[cols, tokens] = ctx[tokens, cols].T

    own_tok, par_tok = pl.ds(0, TOK), pl.ds(TOK, TOK)
    loc_w.wait()
    loc_ctx.wait()
    project(z, own_tok, first=True)
    turn(own_tok)

    stages = (outer_1, outer_2)
    for hop in range(1, 4):
        froms = (chunk_at(-hop), chunk_at(hop))
        for u in range(4):
            for way in range(2):
                arrive(
                    wbuf.at[unit_rows(froms[way], u), :],
                    zs_sem.at[way, hop - 1, u],
                    zr_sem.at[way, hop - 1, u],
                )
                pass_on(hop, u, way, froms[way])
            if hop == 3 and u == 2:
                arrive(ctx.at[par_tok, :], ys_sem.at[2], yr_sem.at[2])
                project(z, par_tok, first=True)
                for near in (1, -1, 2, -2):
                    project(chunk_at(near), par_tok)
        for way in range(2):
            project(froms[way], own_tok)
            if hop == 3:
                project(froms[way], par_tok)
        if hop < 3:
            stages[hop - 1]()

    def project_part(owner, tokens):
        rows = pl.ds(pl.multiple_of(chunk_at(4) * CHUNK + owner * ROWS, ROWS), ROWS)

        @pl.loop(0, 4, unroll=True)
        def _(n):
            cols = pl.ds(aligned(n, 256), 256)
            proj[tokens, cols] += jnp.dot(
                ctx[tokens, rows], wbuf[rows, cols], preferred_element_type=F32
            )

    last = chunk_at(4)
    for u in range(4):
        arrive(wbuf.at[unit_rows(last, u), :], zs_sem.at[u % 2, 3, u], zr_sem.at[u % 2, 3, u])
        if u == 1:
            project_part(y, pl.ds(0, PAIR))
            loc_cot.wait()
            loc_gain.wait()
            arrive(cot.at[par_tok, :], ys_sem.at[3], yr_sem.at[3])

    gain = gain_buf[...]

    def stat_sem(half):
        return 4 if half == 1 else 11

    for half in (1, 0):
        project_part(other, pl.ds(half * TOK, TOK))

        @pl.loop(0, TOK // UNIT, unroll=True)
        def _(r):
            rows = rows_of(half * TOK + r * UNIT, UNIT)
            p = proj[rows, :]
            scaled = cot[rows, :].astype(F32) * gain
            square, cross = p * p, scaled * p
            lanes = [slice(128 * i, 128 * i + 128) for i in range(HALF // 128)]
            stat_own[0, rows, :] = sum(square[:, i] for i in lanes)
            stat_own[1, rows, :] = sum(cross[:, i] for i in lanes)

        for n in range(2):
            turned = stat_own[n, half * TOK : half * TOK + TOK, :].T
            stat_send[half, n : n + 1, :] = jnp.sum(turned, axis=0, keepdims=True)
        k = stat_sem(half)
        send(
            stat_send.at[half],
            stat_recv.at[1 - half, pl.ds(0, 8), :],
            ys_sem.at[k],
            yr_sem.at[k],
            pair,
        )

    outer_3()
    turn(par_tok)
    for half in range(2):
        k = stat_sem(1 - half)
        arrive(stat_recv.at[half, pl.ds(0, 8), :], ys_sem.at[k], yr_sem.at[k])
        stat_recv[half, 0:2, :] += stat_send[half, 0:2, :]
        stat_own[0, half * TOK : half * TOK + TOK, :] = stat_recv[half].T

        @pl.loop(0, TOK // UNIT, unroll=True)
        def _(r):
            rows = rows_of(half * TOK + r * UNIT, UNIT)
            stat = stat_own[0, rows, :] * (1.0 / D)
            inv = lax.rsqrt(stat[:, 0:1] + 1e-06)
            slope = inv * inv * stat[:, 1:2]
            scaled = cot[rows, :].astype(F32) * gain
            pg[rows, :] = (inv * (scaled - proj[rows, :] * slope)).astype(BF16)

    def grad_of(rows, dst):
        @pl.loop(0, 4, unroll=True)
        def _(n):
            cols = pl.ds(aligned(n, 256), 256)
            dst[:, cols] = jnp.dot(ctxt[rows, :], pg[:, cols], preferred_element_type=F32)

    def piece_rows(piece, size, offset=0):
        owner = other if piece == 0 else y
        return pl.ds(pl.multiple_of(owner * ROWS + offset, size), size)

    for piece in range(2):
        owner = other if piece == 0 else y
        rows = pl.ds(pl.multiple_of(chunk_at(4) * CHUNK + owner * ROWS, ROWS), ROWS)
        grad_of(rows, far.at[piece_rows(piece, ROWS), :])
        for way in range(2):
            half_send[way, piece] = far[
                piece_rows(piece, ROWS), way * 512 : way * 512 + 512
            ].astype(BF16)
            send(
                half_send.at[way, piece],
                half_recv.at[way, piece],
                hs_sem.at[way, piece],
                hr_sem.at[way, piece],
                ring[way],
            )

    def back(tokens, cols):
        return lax.dot_general(
            pg[tokens, :], wbuf[cols, :], (((1,), (1,)), ((), ())), preferred_element_type=F32
        )

    for q in range(4):
        @pl.loop(0, 2)
        def _(n):
            cols = pl.ds(pl.multiple_of(q * 512 + n * 256, 256), 256)
            cg_send[:, cols] = back(par_tok, cols).astype(BF16)

        cols = pl.ds(q * 512, 512)
        send(cg_send.at[:, cols], cg_recv.at[:, cols], ys_sem.at[5 + q], yr_sem.at[5 + q], pair)

    for way in range(2):
        grad_of(chunk_rows(3 if way == 0 else -3), parts.at[way, 0])

    def forward(hop, piece, t, way):
        n = 2 * piece + t
        rows = pl.ds(t * UNIT, UNIT)
        src = parts.at[way, 3 - hop]
        own = src[piece_rows(piece, UNIT, t * UNIT), :]
        if hop == 3:
            if t == 0:
                arrive(
                    half_recv.at[way, piece], hs_sem.at[way, piece], hr_sem.at[way, piece]
                )
            cut = slice(way * 512, way * 512 + 512)
            rest = slice(512 - way * 512, 1024 - way * 512)
            full_send[way, 0, n, :, cut] = (
                own[:, cut] + half_recv[way, piece, rows, :].astype(F32)
            ).astype(BF16)
            full_send[way, 0, n, :, rest] = own[:, rest].astype(BF16)
        else:
            arrive(
                full_recv.at[way, 2 - hop, n], fs_sem.at[way, 2 - hop, n], fr_sem.at[way, 2 - hop, n]
            )
            full_send[way, 3 - hop, n] = (
                own + full_recv[way, 2 - hop, n].astype(F32)
            ).astype(BF16)
        send(
            full_send.at[way, 3 - hop, n],
            full_recv.at[way, 3 - hop, n],
            fs_sem.at[way, 3 - hop, n],
            fr_sem.at[way, 3 - hop, n],
            ring[way],
        )

    def own_back():
        @pl.loop(0, NZ)
        def _(n):
            cols = pl.ds(aligned(n, 256), 256)
            cg_own[:, cols] = back(own_tok, cols)

    def finish_back():
        for q in range(4):
            cols = pl.ds(q * 512, 512)
            arrive(cg_recv.at[:, cols], ys_sem.at[5 + q], yr_sem.at[5 + q])

        @pl.loop(0, 16)
        def _(r):
            rows = rows_of(r * 16, 16)
            cg_ref[rows, :] = (cg_own[rows, :] + cg_recv[rows, :].astype(F32)).astype(BF16)

    def next_parts(hop):
        for way in range(2):
            grad_of(chunk_rows(hop if way == 0 else -hop), parts.at[way, 3 - hop])

    def both(hop, piece, t):
        for way in range(2):
            forward(hop, piece, t, way)

    def settle(piece, t):
        n = 2 * piece + t
        rows = pl.ds(t * UNIT, UNIT)
        total = far[piece_rows(piece, UNIT, t * UNIT), :]
        for way in range(2):
            arrive(full_recv.at[way, 2, n], fs_sem.at[way, 2, n], fr_sem.at[way, 2, n])
            total = total + full_recv[way, 2, n].astype(F32)
        if piece == 0:
            y_send[t] = total.astype(BF16)
            send(y_send.at[t], y_recv.at[t], ys_sem.at[9 + t], yr_sem.at[9 + t], pair)
        else:
            grad_ref[rows, pl.ds(mine, HALF)] = total

    def take(t):
        arrive(y_recv.at[t], ys_sem.at[9 + t], yr_sem.at[9 + t])
        grad_ref[t * UNIT : (t + 1) * UNIT, pl.ds(theirs, HALF)] = y_recv[t].astype(F32)

    both(3, 0, 0)
    both(3, 0, 1)
    next_parts(2)
    both(3, 1, 0)
    both(3, 1, 1)
    own_back()
    outer_4()
    both(2, 0, 0)
    both(2, 0, 1)
    next_parts(1)
    both(2, 1, 0)
    outer_5()
    both(1, 0, 0)
    both(1, 0, 1)
    both(2, 1, 1)
    grad_of(chunk_rows(0), far)
    outer_6()
    both(1, 1, 0)
    settle(0, 0)
    finish_back()
    settle(0, 1)
    both(1, 1, 1)
    outer_7()
    settle(1, 0)
    take(0)
    take(1)
    settle(1, 1)
    for copy in sends:
        copy.wait_send()
    out_drift.wait()


def exchange(context, cotangent, gain, weight, frags, step):
    anywhere = pl.BlockSpec(memory_space=pl.ANY)
    in_hbm = pl.BlockSpec(memory_space=pltpu.HBM)
    dma = pltpu.SemaphoreType.DMA
    return pl.pallas_call(
        kernel,
        out_shape=(
            jax.ShapeDtypeStruct((TOK, D), BF16),
            jax.ShapeDtypeStruct((ROWS, D), F32),
            jax.ShapeDtypeStruct((ROWS, D), BF16),
        ),
        in_specs=[
            in_hbm,
            in_hbm,
            in_hbm,
            in_hbm,
            in_hbm,
            pl.BlockSpec(memory_space=pltpu.SMEM),
        ],
        out_specs=(
            pl.BlockSpec(memory_space=pltpu.VMEM),
            pl.BlockSpec(memory_space=pltpu.VMEM),
            anywhere,
        ),
        scratch_shapes=[
            pltpu.VMEM((D, HALF), BF16),
            pltpu.VMEM((PAIR, D), BF16),
            pltpu.VMEM((PAIR, HALF), BF16),
            pltpu.VMEM((1, HALF), F32),
            pltpu.VMEM((PAIR, HALF), F32),
            pltpu.VMEM((PAIR, HALF), BF16),
            pltpu.VMEM((D, PAIR), BF16),
            pltpu.VMEM((2, PAIR, 128), F32),
            pltpu.VMEM((2, 8, TOK), F32),
            pltpu.VMEM((2, 128, TOK), F32),
            pltpu.VMEM((CHUNK, HALF), F32),
            pltpu.VMEM((2, 3, CHUNK, HALF), F32),
            pltpu.VMEM((2, 2, ROWS, 512), BF16),
            pltpu.VMEM((2, 2, ROWS, 512), BF16),
            pltpu.VMEM((2, 3, 4, UNIT, HALF), BF16),
            pltpu.VMEM((2, 3, 4, UNIT, HALF), BF16),
            pltpu.VMEM((2, UNIT, HALF), BF16),
            pltpu.VMEM((2, UNIT, HALF), BF16),
            pltpu.VMEM((TOK, D), F32),
            pltpu.VMEM((TOK, D), BF16),
            pltpu.VMEM((TOK, D), BF16),
            pltpu.VMEM((NFRAG, ROWS, D), BF16),
            pltpu.VMEM((ROWS, D), BF16),
            pltpu.VMEM((64, D), F32),
            pltpu.VMEM((32, D), F32),
            pltpu.VMEM((64, D), BF16),
            pltpu.VMEM((32, D), BF16),
            pltpu.VMEM((16, D), BF16),
            pltpu.VMEM((64, D), BF16),
            pltpu.VMEM((32, D), BF16),
            pltpu.VMEM((16, D), BF16),
            pltpu.VMEM((16, D), BF16),
            pltpu.VMEM((ROWS, D), BF16),
            dma((5,)),
            dma((1,)),
            dma((2, 4, 4)),
            dma((2, 4, 4)),
            dma((12,)),
            dma((12,)),
            dma((2, 2)),
            dma((2, 2)),
            dma((2, 3, 4)),
            dma((2, 3, 4)),
            dma((7,)),
            dma((7,)),
        ],
        compiler_params=pltpu.CompilerParams(
            collective_id=0, has_side_effects=True, vmem_limit_bytes=46 * 2**20
        ),
        cost_estimate=pl.CostEstimate(
            flops=6 * TOK * D * D, bytes_accessed=8 * 2**20, transcendentals=PAIR
        ),
        name="exchange",
    )(*(pltpu.with_memory_space_constraint(a, pltpu.HBM) for a in (context, cotangent, gain, weight, frags)), step)


def finish_kernel(
    step_ref,
    cg_ref,
    grad_ref,
    drift_ref,
    one_ref,
    two_ref,
    weight_ref,
    anchors_ref,
    momenta_ref,
    cg_hbm,
    weight_hbm,
    one_hbm,
    two_hbm,
    anchor_hbm,
    momentum_hbm,
    weight_buf,
    one_buf,
    two_buf,
    anchor_buf,
    momentum_buf,
    sem,
):
    copies = []

    def put(src, dst):
        copy = pltpu.make_async_copy(src, dst, sem.at[len(copies)])
        copy.start()
        copies.append(copy)

    put(cg_ref, cg_hbm)
    step = step_ref[0]
    due = lax.rem(step, NFRAG)
    rate = rate_base + rate_base * jnp.minimum(step, 1000).astype(F32) / 1000.0
    for block in range(2):
        @pl.loop(0, 4)
        def _(r):
            rows = pl.ds(pl.multiple_of(block * 64 + r * 16, 16), 16)
            anchor = anchors_ref[due, rows, :].astype(F32)
            pseudo = anchor - drift_ref[rows, :].astype(F32) / N_ISLAND
            momentum = outer_mu * momenta_ref[due, rows, :] + pseudo
            momentum_buf[rows, :] = momentum
            anchor_buf[rows, :] = (anchor - rate * (pseudo + outer_mu * momentum)).astype(BF16)

        rows = pl.ds(block * 64, 64)
        put(momentum_buf.at[rows, :], momentum_hbm.at[rows, :])
        put(anchor_buf.at[rows, :], anchor_hbm.at[rows, :])
    for block in range(4):
        @pl.loop(0, 2, unroll=True)
        def _(r):
            rows = pl.ds(pl.multiple_of(block * 32 + r * 16, 16), 16)
            first = beta_one * one_ref[0, rows, :] + (1.0 - beta_one) * grad_ref[rows, :]
            grad = grad_ref[rows, :]
            second = beta_two * two_ref[0, rows, :] + (1.0 - beta_two) * grad * grad
            weight = weight_ref[0, rows, :].astype(F32)
            update = first / (jnp.sqrt(second) + adam_eps) + decay_rate * weight
            one_buf[rows, :] = first
            two_buf[rows, :] = second
            weight_buf[rows, :] = (weight - inner_rate * update).astype(BF16)

        rows = pl.ds(block * 32, 32)
        put(one_buf.at[rows, :], one_hbm.at[0, rows, :])
        put(two_buf.at[rows, :], two_hbm.at[0, rows, :])
        put(weight_buf.at[rows, :], weight_hbm.at[0, rows, :])

    for copy in copies:
        copy.wait()


def finish(step, *operands):
    inside = pl.BlockSpec(memory_space=pltpu.VMEM)
    anywhere = pl.BlockSpec(memory_space=pl.ANY)
    return pl.pallas_call(
        finish_kernel,
        out_shape=(
            jax.ShapeDtypeStruct((TOK, D), BF16),
            jax.ShapeDtypeStruct((1, ROWS, D), BF16),
            jax.ShapeDtypeStruct((1, ROWS, D), F32),
            jax.ShapeDtypeStruct((1, ROWS, D), F32),
            jax.ShapeDtypeStruct((ROWS, D), BF16),
            jax.ShapeDtypeStruct((ROWS, D), F32),
        ),
        in_specs=[pl.BlockSpec(memory_space=pltpu.SMEM)] + [inside] * 8,
        out_specs=(anywhere,) * 6,
        scratch_shapes=[
            pltpu.VMEM((ROWS, D), BF16),
            pltpu.VMEM((ROWS, D), F32),
            pltpu.VMEM((ROWS, D), F32),
            pltpu.VMEM((ROWS, D), BF16),
            pltpu.VMEM((ROWS, D), F32),
            pltpu.SemaphoreType.DMA((17,)),
        ],
        compiler_params=pltpu.CompilerParams(vmem_limit_bytes=16 * 2**20),
        cost_estimate=pl.CostEstimate(
            flops=30 * ROWS * D, bytes_accessed=12 * 2**20, transcendentals=ROWS * D
        ),
        name="finish",
    )(step, *operands)


def local(
    context,
    cotangent,
    norm_gain,
    out_weight,
    moment_one,
    moment_two,
    local_frags,
    anchors,
    outer_moment,
    outer_step,
):
    ctx_grad, weight_grad, drift = exchange(
        context, cotangent, norm_gain.reshape(1, D), out_weight, local_frags, outer_step
    )
    return finish(
        outer_step,
        ctx_grad,
        weight_grad,
        drift,
        moment_one,
        moment_two,
        out_weight,
        anchors,
        outer_moment,
    )


def solution(mesh):
    return jax.shard_map(
        local,
        mesh=mesh,
        in_specs=(
            P(("island", "fsdp"), None),
            P(("island", "fsdp"), None),
            P(),
            P("island", "fsdp", None),
            P("island", "fsdp", None),
            P("island", "fsdp", None),
            P("island", None, "fsdp", None),
            P(None, "fsdp", None),
            P(None, "fsdp", None),
            P(),
        ),
        out_specs=(
            P(("island", "fsdp"), None),
            P("island", "fsdp", None),
            P("island", "fsdp", None),
            P("island", "fsdp", None),
            P("fsdp", None),
            P("fsdp", None),
        ),
        check_vma=False,
    )
```
